256 devices in a mesh: sink: 32 (over y_lo, z, core), src: 8 (over y_hi, x).
Axes of the slice: x: 4, y: 4 (y_hi: 2, y_lo: 2; y = y_hi * 2 + y_lo), z: 8, core: 2. Of those that a mesh axis runs over, the one named last changes fastest.
Arguments:
- leaf_pos: float32 [2048, 3, 128], P(('sink', 'src')), may hold values from 0 to 4
- leaf_mass: float32 [2048, 128], P(('sink', 'src')), may hold values from 0.3 to 3
- pair_ids: int32 [32, 8, 2, 256], P('sink', 'src'), may hold values from 0 to 2047, as said below
- pair_count: int32 [32, 8], P('sink', 'src'), may hold values from 1 to 256
Outputs:
- force: float32 [2048, 3, 128], P(('sink', 'src'))
The draws below stay inside these ranges and needn't reach their ends.
Inputs may be any that keep to these rules, and one draw needn't show every extreme that they name: `pair_ids`: in list (s, r) every sink leaf id lies in [s * 8 * 8, (s + 1) * 8 * 8), every source leaf id equals (t * 8 + r) * 8 + k for some t and k < 8, and a slot's two ids differ; dead slots also hold such ids.
All inputs are finite; a program needn't handle non-finite values.
Results may differ from the reference program's by a relative error of at most 0.0001.
Values sent between devices are 32-bit elements; how exact they have to be, the bound alone decides.
A program may use at most 64 MiB of HBM per device.

```python
import math
import jax
import jax.numpy as jnp
from jax import lax

LEAF_SIZE = 128
LEAF_DEV = 8
PAIR_CAP = 256
LEAVES = 2048
N_SINK = 32
N_SRC = 8


def draw_pair_ids(key, part):
    key = jax.random.fold_in(key, 11)
    first, second, third = jax.random.split(key, 3)
    shape = (N_SINK, N_SRC, PAIR_CAP)
    row_index = jnp.arange(N_SINK, dtype=jnp.int32)[:, None, None]
    column_index = jnp.arange(N_SRC, dtype=jnp.int32)[None, :, None]
    row_span = N_SRC * LEAF_DEV
    sink_ids = row_index * row_span + jax.random.randint(first, shape, 0, row_span, dtype=jnp.int32)
    owner_row = jax.random.randint(second, shape, 0, N_SINK, dtype=jnp.int32)
    within = jax.random.randint(third, shape, 0, LEAF_DEV, dtype=jnp.int32)
    base = (owner_row * N_SRC + column_index) * LEAF_DEV
    source_ids = base + within
    source_ids = jnp.where(source_ids == sink_ids, base + (within + 1) % LEAF_DEV, source_ids)
    return jnp.stack([sink_ids, source_ids], axis=2).astype(jnp.int32)


def draw_pair_count(key, part):
    key = jax.random.fold_in(key, 23)
    first, second, third = jax.random.split(key, 3)
    shape = (N_SINK * N_SRC,)
    upper = jax.random.randint(first, shape, 0, PAIR_CAP, dtype=jnp.int32)
    lower = jax.random.randint(second, shape, 0, PAIR_CAP, dtype=jnp.int32)
    counts = 1 + upper * lower // PAIR_CAP
    chosen = jax.random.randint(third, (), 0, N_SINK * N_SRC, dtype=jnp.int32)
    counts = jnp.where(jnp.arange(N_SINK * N_SRC, dtype=jnp.int32) == chosen, PAIR_CAP, counts)
    return counts.reshape(N_SINK, N_SRC).astype(jnp.int32)


def block_levels(stream_key, dims, shards, low, top_value):
    factor_of = 1.0
    for position, blocks in shards:
        draws = jax.random.uniform(jax.random.fold_in(jax.random.fold_in(stream_key, 6), position), (blocks,), jnp.float32, low / len(shards), top_value / len(shards))
        factor_of = factor_of * jnp.repeat(jnp.exp(draws), dims[position] // blocks).reshape((-1,) + (1,) * (len(dims) - 1 - position))
    return factor_of


def setup_inputs(seed: int = 0) -> dict:
    key_list = jax.random.split(jax.random.key(seed), 5)
    return {
        "leaf_pos": jnp.clip(4.0 * jax.random.uniform(key_list[0], (LEAVES, 3, LEAF_SIZE), jnp.float32) ** block_levels(key_list[0], (LEAVES, 3, LEAF_SIZE), ((0, 256),), -0.2, 0.2), 0.0, 4.0),
        "leaf_mass": jnp.clip(jnp.exp(math.log(3.0) - 2.3025851 * jax.random.uniform(key_list[1], (LEAVES, LEAF_SIZE), jnp.float32) ** block_levels(key_list[1], (LEAVES, LEAF_SIZE), ((0, 256),), -0.2, 0.2)), 0.3, 3.0),
        "pair_ids": draw_pair_ids(jax.random.fold_in(key_list[4], 71), 0),
        "pair_count": draw_pair_count(jax.random.fold_in(key_list[4], 71), 0),
    }


SOFTEN = 0.09
SPLIT_SCALE = 1.25
GRAVITY = 0.05
TWO_ROOT_PI = 1.1283791670955126

def pair_forces(sink_pos, sink_mass, source_pos, source_mass, live_mask):
    offset = source_pos[:, :, None, :] - sink_pos[:, :, :, None]
    dist_sq = lax.optimization_barrier(jnp.sum(offset * offset, axis=1)) + SOFTEN
    distance = jnp.sqrt(dist_sq)
    scaled = distance * (0.5 / SPLIT_SCALE)
    shaping = jax.scipy.special.erfc(scaled) + TWO_ROOT_PI * scaled * jnp.exp(-scaled * scaled)
    weight_ij = GRAVITY * shaping / (dist_sq * distance)
    weight_ij = weight_ij * sink_mass[:, :, None] * source_mass[:, None, :] * live_mask[:, None, None]
    pulled = weight_ij[:, None, :, :] * offset
    return (lax.optimization_barrier(jnp.sum(pulled, axis=3)), -lax.optimization_barrier(jnp.sum(pulled, axis=2)))

def reference(leaf_pos, leaf_mass, pair_ids, pair_count):
    lists = N_SINK * N_SRC
    sink_ids = pair_ids[:, :, 0, :].reshape(lists, PAIR_CAP).astype(jnp.int32)
    source_ids = pair_ids[:, :, 1, :].reshape(lists, PAIR_CAP).astype(jnp.int32)
    slots = jnp.arange(PAIR_CAP, dtype=jnp.int32)
    live_mask = (slots[None, :] < pair_count.reshape(lists, 1).astype(jnp.int32)).astype(jnp.float32)

    def visit(total, block):
        sinks_here, sources_here, live_here = block
        force_sink, force_source = pair_forces(leaf_pos[sinks_here], leaf_mass[sinks_here], leaf_pos[sources_here], leaf_mass[sources_here], live_here)
        total = total.at[sinks_here].add(force_sink).at[sources_here].add(force_source)
        return (total, None)
    start = jnp.zeros((LEAVES, 3, LEAF_SIZE), jnp.float32)
    total, ignored = lax.scan(visit, start, (sink_ids, source_ids, live_mask))
    return total
```

```python
import functools
import math

import jax
import jax.numpy as jnp
from jax import lax
from jax.experimental import pallas as pl
from jax.experimental.pallas import tpu as pltpu
from jax.sharding import PartitionSpec as P

F32 = jnp.float32
BF16 = jnp.bfloat16
SOFTEN = 0.09
LEAF_DEV = 8
CELLS = 128
PAIR_CAP = 256
FIELDS = 32
FORCES = 24
UNROLL = 4
SHAPE = (
    -4.38650632,
    -1.564356609,
    -0.03132662886,
    -0.009803538989,
    -0.002175578276,
    -0.000355445319,
    -4.231931911e-05,
    -3.170157177e-06,
    -1.052514463e-07,
    -2.359194952e-08,
    -4.944213016e-09,
)


def pair_weight(dist_sq):
    scale = jnp.log(dist_sq) * (1.0 / math.log(2.0))
    total = scale * SHAPE[-1] + SHAPE[-2]
    for coef in SHAPE[-3::-1]:
        total = total * scale + coef
    return jnp.exp2(total)


def place():
    return lax.axis_index("sink"), lax.axis_index("src")


def greet(peers):
    barrier = pltpu.get_barrier_semaphore()
    for peer in peers:
        pl.semaphore_signal(
            barrier, inc=1, device_id=peer, device_id_type=pl.DeviceIdType.MESH
        )
    pl.semaphore_wait(barrier, len(peers))


def neighbours(chips, group):
    sink, src = place()
    core = lax.rem(sink, 2)
    chip = sink // 2
    partner = (sink + 1 - 2 * core, src)
    column = [(lax.rem(chip + o, chips) * 2 + core, src) for o in range(1, chips)]
    row = [(sink, lax.rem(src + o, group)) for o in range(1, group)]
    return sink, src, core, chip, partner, column, row


def remote(source, target, send, recv, device):
    return pltpu.make_async_remote_copy(
        src_ref=source,
        dst_ref=target,
        send_sem=send,
        recv_sem=recv,
        device_id=device,
        device_id_type=pl.DeviceIdType.MESH,
    )


def gather_kernel(
    chips, group, pos, mass, ids, count, column_out, rows_out, ids_out,
    pack, column_send, column_recv, row_send, row_recv,
    pass_send, pass_recv, hand_send, hand_recv, own_send, own_recv,
):
    sink, src, core, chip, partner, column, row = neighbours(chips, group)
    greet(column + row + [partner])
    for c in range(3):
        pack[c * 8 : c * 8 + 8, :] = pos[:, c, :]
    pack[24:32, :] = mass[...]
    ids_out[core, 0:2, :] = ids[0, 0, :, 0:128]
    ids_out[core, 2:4, :] = ids[0, 0, :, 128:256]
    ids_out[core, 4:8, :] = jnp.full((4, 128), count[0, 0], jnp.int32)

    sends = []

    def start(copy):
        copy.start()
        sends.append(copy)

    for o, peer in enumerate(column):
        start(remote(pack, column_out.at[sink], column_send.at[o], column_recv.at[o], peer))
    for o, peer in enumerate(row):
        start(remote(pack, rows_out.at[core, src], row_send.at[o], row_recv.at[o], peer))
    start(remote(pack, column_out.at[sink], own_send.at[0], own_recv.at[0], partner))
    start(remote(pack, rows_out.at[core, src], own_send.at[1], own_recv.at[1], partner))
    start(remote(ids_out.at[core], ids_out.at[core], own_send.at[2], own_recv.at[2], partner))
    column_out[sink] = pack[...]
    rows_out[core, src] = pack[...]

    for o in range(1, chips):
        origin = lax.rem(chip + chips - o, chips) * 2 + core
        block = column_out.at[origin]
        remote(pack, block, column_send.at[o - 1], column_recv.at[o - 1], partner).wait_recv()
        start(remote(block, block, pass_send.at[o - 1], pass_recv.at[o - 1], partner))
    for o in range(1, group):
        origin = lax.rem(src + group - o, group)
        block = rows_out.at[core, origin]
        remote(pack, block, row_send.at[o - 1], row_recv.at[o - 1], partner).wait_recv()
        start(remote(block, block, hand_send.at[o - 1], hand_recv.at[o - 1], partner))

    other = 1 - core
    for o in range(1, chips):
        origin = lax.rem(chip + chips - o, chips) * 2 + other
        remote(pack, column_out.at[origin], pass_send.at[o - 1], pass_recv.at[o - 1], partner).wait_recv()
    for o in range(1, group):
        origin = lax.rem(src + group - o, group)
        remote(pack, rows_out.at[other, origin], hand_send.at[o - 1], hand_recv.at[o - 1], partner).wait_recv()
    there = chip * 2 + other
    remote(pack, column_out.at[there], own_send.at[0], own_recv.at[0], partner).wait_recv()
    remote(pack, rows_out.at[other, src], own_send.at[1], own_recv.at[1], partner).wait_recv()
    remote(ids_out.at[other], ids_out.at[other], own_send.at[2], own_recv.at[2], partner).wait_recv()
    for copy in sends:
        copy.wait_send()


def pair_kernel(chips, group, ids, rows, column, row_force, column_force, parts, choose, acc, first_x, second_x):
    blocks = 2 * group
    core = lax.rem(lax.axis_index("sink"), 2)
    column_force[...] = jnp.zeros_like(column_force)
    for h in range(blocks):
        block = rows[h // group, h % group]
        high = block.astype(BF16).astype(F32)
        rest = block - high
        middle = rest.astype(BF16).astype(F32)
        low = rest - middle
        stacked = jnp.concatenate([high, middle, low, jnp.zeros_like(high)], axis=0)
        parts[h] = stacked.T.astype(BF16)
    depth = lax.broadcasted_iota(jnp.int32, (128, 512), 0)
    field = lax.broadcasted_iota(jnp.int32, (128, 512), 1) // 128
    hit = (depth < 96) & (depth % 32 // 8 == field)
    for k in range(8):
        choose[k] = jnp.where(hit & (depth % 8 == k), 1.0, 0.0).astype(BF16)
    for g in range(blocks // 4):
        acc[g] = jnp.zeros((128, 128), F32)
    lane = lax.broadcasted_iota(jnp.int32, (8, 128), 1)

    count_0 = ids[0, 4, 0]
    both = count_0 + ids[1, 4, 0]
    half = (both + 1) // 2
    begin = jnp.where(core == 0, 0, half)
    end = jnp.where(core == 0, half, both)

    def look(slot):
        slot = jnp.minimum(slot, both - 1)
        which = jnp.where(slot < count_0, 0, 1)
        p = slot - which * count_0
        a = ids[which, p // 128 * 2, p % 128]
        b = ids[which, p // 128 * 2 + 1, p % 128]
        sink_block = which * group + a // LEAF_DEV % group
        return sink_block, a % LEAF_DEV, b // (LEAF_DEV * group), b % LEAF_DEV

    def fill(target, first):
        for u in range(UNROLL):
            sink_block, k, _, _ = look(first + u)
            target[u] = jnp.dot(parts[sink_block], choose[k], preferred_element_type=F32)

    def use(spread, first):
        done = []
        for u in range(UNROLL):
            sink_block, k, source_block, source_k = look(first + u)
            live = jnp.where(first + u < end, 1.0, 0.0)
            at = sink_block % 4 * 32 + k
            here = [
                jnp.broadcast_to(column[source_block, pl.ds(8 * c + source_k, 1), :], (8, 128))
                for c in range(4)
            ]
            mass = here[3] * live
            masks = [lane == at + 8 * c for c in range(3)]
            source_sum = [jnp.zeros((8, 128), F32) for _ in range(3)]
            sink_sum = []
            for i in range(0, CELLS, 8):
                there = [spread[u, i : i + 8, 128 * c : 128 * c + 128] for c in range(4)]
                offset = [here[c] - there[c] for c in range(3)]
                dist_sq = (offset[0] * offset[0] + offset[1] * offset[1]) + (
                    offset[2] * offset[2] + SOFTEN
                )
                weight = (pair_weight(dist_sq) * there[3]) * mass
                force = [weight * offset[c] for c in range(3)]
                source_sum = [source_sum[c] + force[c] for c in range(3)]
                total = [jnp.sum(force[c], axis=1, keepdims=True) for c in range(3)]
                sink_sum.append(
                    jnp.where(
                        masks[0],
                        total[0],
                        jnp.where(masks[1], total[1], jnp.where(masks[2], total[2], 0.0)),
                    )
                )
            done.append((sink_block // 4, source_block, source_k, source_sum, sink_sum))
        for g, source_block, source_k, source_sum, sink_sum in done:
            for i, value in enumerate(sink_sum):
                acc[g, pl.ds(8 * i, 8), :] += value
            slot = source_block % 2 * chips + source_block // 2
            for c in range(3):
                column_force[slot, pl.ds(8 * c + source_k, 1), :] -= jnp.sum(
                    source_sum[c], axis=0, keepdims=True
                )

    fill(first_x, begin)

    def turn(i, carry):
        first = begin + i * (2 * UNROLL)
        fill(second_x, first + UNROLL)
        use(first_x, first)
        fill(first_x, first + 2 * UNROLL)
        use(second_x, first + UNROLL)
        return carry

    lax.fori_loop(0, (end - begin + 2 * UNROLL - 1) // (2 * UNROLL), turn, 0)
    for g in range(blocks // 4):
        turned = acc[g].T
        for h in range(4):
            block = g * 4 + h
            row_force[block // group, block % group] = turned[32 * h : 32 * h + FORCES, :]


def reduce_kernel(
    chips, group, row_force, column_force, out,
    row_sum, column_sum, row_in, column_in, swap_row, swap_column,
    column_send, column_recv, row_send, row_recv, swap_send, swap_recv,
):
    sink, src, core, chip, partner, column, row = neighbours(chips, group)
    other = 1 - core
    greet(column + row + [partner])
    to_column = remote(
        column_force.at[pl.ds(other * chips, chips)], swap_column,
        swap_send.at[0], swap_recv.at[0], partner,
    )
    to_row = remote(row_force.at[other], swap_row, swap_send.at[1], swap_recv.at[1], partner)
    to_column.start()
    to_row.start()
    to_column.wait_recv()
    column_sum[...] = column_force[pl.ds(core * chips, chips)] + swap_column[...]
    sends = [to_column, to_row]
    for o, peer in enumerate(column):
        target = lax.rem(chip + o + 1, chips)
        copy = remote(column_sum.at[target], column_in.at[o], column_send.at[o], column_recv.at[o], peer)
        copy.start()
        sends.append(copy)
    to_row.wait_recv()
    row_sum[...] = row_force[core] + swap_row[...]
    for o, peer in enumerate(row):
        target = lax.rem(src + o + 1, group)
        copy = remote(row_sum.at[target], row_in.at[o], row_send.at[o], row_recv.at[o], peer)
        copy.start()
        sends.append(copy)
    total = column_sum[chip] + row_sum[src]
    for o in range(group - 1):
        remote(row_sum.at[0], row_in.at[o], row_send.at[o], row_recv.at[o], partner).wait_recv()
        total = total + row_in[o]
    for o in range(chips - 1):
        remote(column_sum.at[0], column_in.at[o], column_send.at[o], column_recv.at[o], partner).wait_recv()
        total = total + column_in[o]
    for c in range(3):
        out[:, c, :] = total[8 * c : 8 * c + 8, :]
    for copy in sends:
        copy.wait_send()


def per_device(chips, group, leaf_pos, leaf_mass, pair_ids, pair_count):
    vmem = pl.BlockSpec(memory_space=pltpu.VMEM)
    smem = pl.BlockSpec(memory_space=pltpu.SMEM)
    dma = pltpu.SemaphoreType.DMA
    column, rows, ids = pl.pallas_call(
        functools.partial(gather_kernel, chips, group),
        name="gather",
        out_shape=(
            jax.ShapeDtypeStruct((2 * chips, FIELDS, CELLS), F32),
            jax.ShapeDtypeStruct((2, group, FIELDS, CELLS), F32),
            jax.ShapeDtypeStruct((2, 8, CELLS), jnp.int32),
        ),
        in_specs=[vmem, vmem, vmem, smem],
        out_specs=(vmem, vmem, vmem),
        scratch_shapes=[
            pltpu.VMEM((FIELDS, CELLS), F32),
            dma((chips - 1,)), dma((chips - 1,)),
            dma((group - 1,)), dma((group - 1,)),
            dma((chips - 1,)), dma((chips - 1,)),
            dma((group - 1,)), dma((group - 1,)),
            dma((3,)), dma((3,)),
        ],
        compiler_params=pltpu.CompilerParams(
            collective_id=0, has_side_effects=True, vmem_limit_bytes=16 << 20
        ),
    )(leaf_pos, leaf_mass, pair_ids, pair_count)
    blocks = 2 * group
    row_force, column_force = pl.pallas_call(
        functools.partial(pair_kernel, chips, group),
        name="pairs",
        out_shape=(
            jax.ShapeDtypeStruct((2, group, FORCES, CELLS), F32),
            jax.ShapeDtypeStruct((2 * chips, FORCES, CELLS), F32),
        ),
        in_specs=[smem, vmem, vmem],
        out_specs=(vmem, vmem),
        scratch_shapes=[
            pltpu.VMEM((blocks, 128, 128), BF16),
            pltpu.VMEM((8, 128, 512), BF16),
            pltpu.VMEM((blocks // 4, 128, 128), F32),
            pltpu.VMEM((UNROLL, 128, 512), F32),
            pltpu.VMEM((UNROLL, 128, 512), F32),
        ],
        compiler_params=pltpu.CompilerParams(vmem_limit_bytes=40 << 20),
    )(ids, rows, column)
    return pl.pallas_call(
        functools.partial(reduce_kernel, chips, group),
        name="reduce",
        out_shape=jax.ShapeDtypeStruct((LEAF_DEV, 3, CELLS), F32),
        in_specs=[vmem, vmem],
        out_specs=vmem,
        scratch_shapes=[
            pltpu.VMEM((group, FORCES, CELLS), F32),
            pltpu.VMEM((chips, FORCES, CELLS), F32),
            pltpu.VMEM((group - 1, FORCES, CELLS), F32),
            pltpu.VMEM((chips - 1, FORCES, CELLS), F32),
            pltpu.VMEM((group, FORCES, CELLS), F32),
            pltpu.VMEM((chips, FORCES, CELLS), F32),
            dma((chips - 1,)), dma((chips - 1,)),
            dma((group - 1,)), dma((group - 1,)),
            dma((2,)), dma((2,)),
        ],
        compiler_params=pltpu.CompilerParams(
            collective_id=1, has_side_effects=True, vmem_limit_bytes=16 << 20
        ),
    )(row_force, column_force)


def solution(mesh):
    return jax.shard_map(
        functools.partial(per_device, mesh.shape["sink"] // 2, mesh.shape["src"]),
        mesh=mesh,
        in_specs=(
            P(("sink", "src"), None, None),
            P(("sink", "src"), None),
            P("sink", "src", None, None),
            P("sink", "src"),
        ),
        out_specs=P(("sink", "src"), None, None),
        check_vma=False,
    )
```

```python
import functools
import math

import jax
import jax.numpy as jnp
from jax import lax
from jax.experimental import pallas as pl
from jax.experimental.pallas import tpu as pltpu
from jax.sharding import PartitionSpec as P

F32 = jnp.float32
BF16 = jnp.bfloat16
SOFTEN = 0.09
LEAF_DEV = 8
CELLS = 128
PAIR_CAP = 256
FIELDS = 32
FORCES = 24
UNROLL = 4
GRAVITY = 0.05
FALLOFF = 0.16
TWO_ROOT_PI = 1.1283791670955126
FACTOR = GRAVITY * FALLOFF**1.5


def pair_weight(dist_sq):
    square = dist_sq * FALLOFF
    inverse = lax.rsqrt(square)
    tail = 1.0 - lax.erf(square * inverse)
    bell = jnp.exp2(dist_sq * (-FALLOFF / math.log(2.0)))
    return (tail * inverse + bell * TWO_ROOT_PI) * (inverse * inverse)


def place():
    return lax.axis_index("sink"), lax.axis_index("src")


def greet(peers):
    barrier = pltpu.get_barrier_semaphore()
    for peer in peers:
        pl.semaphore_signal(
            barrier, inc=1, device_id=peer, device_id_type=pl.DeviceIdType.MESH
        )
    pl.semaphore_wait(barrier, len(peers))


def neighbours(chips, group):
    sink, src = place()
    core = lax.rem(sink, 2)
    chip = sink // 2
    partner = (sink + 1 - 2 * core, src)
    column = [(lax.rem(chip + o, chips) * 2 + core, src) for o in range(1, chips)]
    row = [(sink, lax.rem(src + o, group)) for o in range(1, group)]
    return sink, src, core, chip, partner, column, row


def remote(source, target, send, recv, device):
    return pltpu.make_async_remote_copy(
        src_ref=source,
        dst_ref=target,
        send_sem=send,
        recv_sem=recv,
        device_id=device,
        device_id_type=pl.DeviceIdType.MESH,
    )


def gather_kernel(
    chips, group, pos, mass, ids, count, column_out, rows_out, ids_out,
    pack, column_send, column_recv, row_send, row_recv,
    pass_send, pass_recv, hand_send, hand_recv, own_send, own_recv,
):
    sink, src, core, chip, partner, column, row = neighbours(chips, group)
    greet(column + row + [partner])
    for c in range(3):
        pack[c * 8 : c * 8 + 8, :] = pos[:, c, :]
    pack[24:32, :] = mass[...]
    ids_out[core, 0:2, :] = ids[0, 0, :, 0:128]
    ids_out[core, 2:4, :] = ids[0, 0, :, 128:256]
    ids_out[core, 4:8, :] = jnp.full((4, 128), count[0, 0], jnp.int32)

    sends = []

    def start(copy):
        copy.start()
        sends.append(copy)

    for o, peer in enumerate(column):
        start(remote(pack, column_out.at[sink], column_send.at[o], column_recv.at[o], peer))
    for o, peer in enumerate(row):
        start(remote(pack, rows_out.at[core, src], row_send.at[o], row_recv.at[o], peer))
    start(remote(pack, column_out.at[sink], own_send.at[0], own_recv.at[0], partner))
    start(remote(pack, rows_out.at[core, src], own_send.at[1], own_recv.at[1], partner))
    start(remote(ids_out.at[core], ids_out.at[core], own_send.at[2], own_recv.at[2], partner))
    column_out[sink] = pack[...]
    rows_out[core, src] = pack[...]

    for o in range(1, chips):
        origin = lax.rem(chip + chips - o, chips) * 2 + core
        block = column_out.at[origin]
        remote(pack, block, column_send.at[o - 1], column_recv.at[o - 1], partner).wait_recv()
        start(remote(block, block, pass_send.at[o - 1], pass_recv.at[o - 1], partner))
    for o in range(1, group):
        origin = lax.rem(src + group - o, group)
        block = rows_out.at[core, origin]
        remote(pack, block, row_send.at[o - 1], row_recv.at[o - 1], partner).wait_recv()
        start(remote(block, block, hand_send.at[o - 1], hand_recv.at[o - 1], partner))

    other = 1 - core
    for o in range(1, chips):
        origin = lax.rem(chip + chips - o, chips) * 2 + other
        remote(pack, column_out.at[origin], pass_send.at[o - 1], pass_recv.at[o - 1], partner).wait_recv()
    for o in range(1, group):
        origin = lax.rem(src + group - o, group)
        remote(pack, rows_out.at[other, origin], hand_send.at[o - 1], hand_recv.at[o - 1], partner).wait_recv()
    there = chip * 2 + other
    remote(pack, column_out.at[there], own_send.at[0], own_recv.at[0], partner).wait_recv()
    remote(pack, rows_out.at[other, src], own_send.at[1], own_recv.at[1], partner).wait_recv()
    remote(ids_out.at[other], ids_out.at[other], own_send.at[2], own_recv.at[2], partner).wait_recv()
    for copy in sends:
        copy.wait_send()


def pair_kernel(chips, group, ids, rows, column, row_force, column_force, parts, choose, acc, first_x, second_x):
    blocks = 2 * group
    core = lax.rem(lax.axis_index("sink"), 2)
    column_force[...] = jnp.zeros_like(column_force)
    for h in range(blocks):
        block = rows[h // group, h % group]
        high = block.astype(BF16).astype(F32)
        rest = block - high
        middle = rest.astype(BF16).astype(F32)
        low = rest - middle
        stacked = jnp.concatenate([high, middle, low, jnp.zeros_like(high)], axis=0)
        parts[h] = stacked.T.astype(BF16)
    depth = lax.broadcasted_iota(jnp.int32, (128, 512), 0)
    field = lax.broadcasted_iota(jnp.int32, (128, 512), 1) // 128
    hit = (depth < 96) & (depth % 32 // 8 == field)
    for k in range(8):
        choose[k] = jnp.where(hit & (depth % 8 == k), 1.0, 0.0).astype(BF16)
    for g in range(blocks // 4):
        acc[g] = jnp.zeros((128, 128), F32)
    lane = lax.broadcasted_iota(jnp.int32, (8, 128), 1)

    count_0 = ids[0, 4, 0]
    both = count_0 + ids[1, 4, 0]
    half = (both + 1) // 2
    begin = jnp.where(core == 0, 0, half)
    end = jnp.where(core == 0, half, both)

    def look(slot):
        slot = jnp.minimum(slot, both - 1)
        which = jnp.where(slot < count_0, 0, 1)
        p = slot - which * count_0
        a = ids[which, p // 128 * 2, p % 128]
        b = ids[which, p // 128 * 2 + 1, p % 128]
        sink_block = which * group + a // LEAF_DEV % group
        return sink_block, a % LEAF_DEV, b // (LEAF_DEV * group), b % LEAF_DEV

    def fill(target, first):
        for u in range(UNROLL):
            sink_block, k, _, _ = look(first + u)
            target[u] = jnp.dot(parts[sink_block], choose[k], preferred_element_type=F32)

    def use(spread, first):
        done = []
        for u in range(UNROLL):
            sink_block, k, source_block, source_k = look(first + u)
            live = jnp.where(first + u < end, FACTOR, 0.0)
            at = sink_block % 4 * 32 + k
            here = [
                jnp.broadcast_to(column[source_block, pl.ds(8 * c + source_k, 1), :], (8, 128))
                for c in range(4)
            ]
            mass = here[3] * live
            masks = [lane == at + 8 * c for c in range(3)]
            source_sum = [jnp.zeros((8, 128), F32) for _ in range(3)]
            sink_sum = []
            for i in range(0, CELLS, 8):
                there = [spread[u, i : i + 8, 128 * c : 128 * c + 128] for c in range(4)]
                offset = [here[c] - there[c] for c in range(3)]
                dist_sq = (offset[0] * offset[0] + offset[1] * offset[1]) + (
                    offset[2] * offset[2] + SOFTEN
                )
                weight = (pair_weight(dist_sq) * there[3]) * mass
                force = [weight * offset[c] for c in range(3)]
                source_sum = [source_sum[c] + force[c] for c in range(3)]
                total = [jnp.sum(force[c], axis=1, keepdims=True) for c in range(3)]
                sink_sum.append(
                    jnp.where(
                        masks[0],
                        total[0],
                        jnp.where(masks[1], total[1], jnp.where(masks[2], total[2], 0.0)),
                    )
                )
            done.append((sink_block // 4, source_block, source_k, source_sum, sink_sum))
        for g, source_block, source_k, source_sum, sink_sum in done:
            for i, value in enumerate(sink_sum):
                acc[g, pl.ds(8 * i, 8), :] += value
            slot = source_block % 2 * chips + source_block // 2
            for c in range(3):
                column_force[slot, pl.ds(8 * c + source_k, 1), :] -= jnp.sum(
                    source_sum[c], axis=0, keepdims=True
                )

    fill(first_x, begin)

    def turn(i, carry):
        first = begin + i * (2 * UNROLL)
        fill(second_x, first + UNROLL)
        use(first_x, first)
        fill(first_x, first + 2 * UNROLL)
        use(second_x, first + UNROLL)
        return carry

    lax.fori_loop(0, (end - begin + 2 * UNROLL - 1) // (2 * UNROLL), turn, 0)
    for g in range(blocks // 4):
        turned = acc[g].T
        for h in range(4):
            block = g * 4 + h
            row_force[block // group, block % group] = turned[32 * h : 32 * h + FORCES, :]


def reduce_kernel(
    chips, group, row_force, column_force, out,
    row_sum, column_sum, row_in, column_in, swap_row, swap_column,
    column_send, column_recv, row_send, row_recv, swap_send, swap_recv,
):
    sink, src, core, chip, partner, column, row = neighbours(chips, group)
    other = 1 - core
    greet(column + row + [partner])
    to_column = remote(
        column_force.at[pl.ds(other * chips, chips)], swap_column,
        swap_send.at[0], swap_recv.at[0], partner,
    )
    to_row = remote(row_force.at[other], swap_row, swap_send.at[1], swap_recv.at[1], partner)
    to_column.start()
    to_row.start()
    to_column.wait_recv()
    column_sum[...] = column_force[pl.ds(core * chips, chips)] + swap_column[...]
    sends = [to_column, to_row]
    for o, peer in enumerate(column):
        target = lax.rem(chip + o + 1, chips)
        copy = remote(column_sum.at[target], column_in.at[o], column_send.at[o], column_recv.at[o], peer)
        copy.start()
        sends.append(copy)
    to_row.wait_recv()
    row_sum[...] = row_force[core] + swap_row[...]
    for o, peer in enumerate(row):
        target = lax.rem(src + o + 1, group)
        copy = remote(row_sum.at[target], row_in.at[o], row_send.at[o], row_recv.at[o], peer)
        copy.start()
        sends.append(copy)
    total = column_sum[chip] + row_sum[src]
    for o in range(group - 1):
        remote(row_sum.at[0], row_in.at[o], row_send.at[o], row_recv.at[o], partner).wait_recv()
        total = total + row_in[o]
    for o in range(chips - 1):
        remote(column_sum.at[0], column_in.at[o], column_send.at[o], column_recv.at[o], partner).wait_recv()
        total = total + column_in[o]
    for c in range(3):
        out[:, c, :] = total[8 * c : 8 * c + 8, :]
    for copy in sends:
        copy.wait_send()


def per_device(chips, group, leaf_pos, leaf_mass, pair_ids, pair_count):
    vmem = pl.BlockSpec(memory_space=pltpu.VMEM)
    smem = pl.BlockSpec(memory_space=pltpu.SMEM)
    dma = pltpu.SemaphoreType.DMA
    column, rows, ids = pl.pallas_call(
        functools.partial(gather_kernel, chips, group),
        name="gather",
        out_shape=(
            jax.ShapeDtypeStruct((2 * chips, FIELDS, CELLS), F32),
            jax.ShapeDtypeStruct((2, group, FIELDS, CELLS), F32),
            jax.ShapeDtypeStruct((2, 8, CELLS), jnp.int32),
        ),
        in_specs=[vmem, vmem, vmem, smem],
        out_specs=(vmem, vmem, vmem),
        scratch_shapes=[
            pltpu.VMEM((FIELDS, CELLS), F32),
            dma((chips - 1,)), dma((chips - 1,)),
            dma((group - 1,)), dma((group - 1,)),
            dma((chips - 1,)), dma((chips - 1,)),
            dma((group - 1,)), dma((group - 1,)),
            dma((3,)), dma((3,)),
        ],
        compiler_params=pltpu.CompilerParams(
            collective_id=0, has_side_effects=True, vmem_limit_bytes=16 << 20
        ),
    )(leaf_pos, leaf_mass, pair_ids, pair_count)
    blocks = 2 * group
    row_force, column_force = pl.pallas_call(
        functools.partial(pair_kernel, chips, group),
        name="pairs",
        out_shape=(
            jax.ShapeDtypeStruct((2, group, FORCES, CELLS), F32),
            jax.ShapeDtypeStruct((2 * chips, FORCES, CELLS), F32),
        ),
        in_specs=[smem, vmem, vmem],
        out_specs=(vmem, vmem),
        scratch_shapes=[
            pltpu.VMEM((blocks, 128, 128), BF16),
            pltpu.VMEM((8, 128, 512), BF16),
            pltpu.VMEM((blocks // 4, 128, 128), F32),
            pltpu.VMEM((UNROLL, 128, 512), F32),
            pltpu.VMEM((UNROLL, 128, 512), F32),
        ],
        compiler_params=pltpu.CompilerParams(vmem_limit_bytes=40 << 20),
    )(ids, rows, column)
    return pl.pallas_call(
        functools.partial(reduce_kernel, chips, group),
        name="reduce",
        out_shape=jax.ShapeDtypeStruct((LEAF_DEV, 3, CELLS), F32),
        in_specs=[vmem, vmem],
        out_specs=vmem,
        scratch_shapes=[
            pltpu.VMEM((group, FORCES, CELLS), F32),
            pltpu.VMEM((chips, FORCES, CELLS), F32),
            pltpu.VMEM((group - 1, FORCES, CELLS), F32),
            pltpu.VMEM((chips - 1, FORCES, CELLS), F32),
            pltpu.VMEM((group, FORCES, CELLS), F32),
            pltpu.VMEM((chips, FORCES, CELLS), F32),
            dma((chips - 1,)), dma((chips - 1,)),
            dma((group - 1,)), dma((group - 1,)),
            dma((2,)), dma((2,)),
        ],
        compiler_params=pltpu.CompilerParams(
            collective_id=1, has_side_effects=True, vmem_limit_bytes=16 << 20
        ),
    )(row_force, column_force)


def solution(mesh):
    return jax.shard_map(
        functools.partial(per_device, mesh.shape["sink"] // 2, mesh.shape["src"]),
        mesh=mesh,
        in_specs=(
            P(("sink", "src"), None, None),
            P(("sink", "src"), None),
            P("sink", "src", None, None),
            P("sink", "src"),
        ),
        out_specs=P(("sink", "src"), None, None),
        check_vma=False,
    )
```

```python
import functools
import math

import jax
import jax.numpy as jnp
from jax import lax
from jax.experimental import pallas as pl
from jax.experimental.pallas import tpu as pltpu
from jax.sharding import PartitionSpec as P

F32 = jnp.float32
BF16 = jnp.bfloat16
SOFTEN = 0.09
LEAF_DEV = 8
CELLS = 128
PAIR_CAP = 256
FIELDS = 32
FORCES = 24
UNROLL = 4
GRAVITY = 0.05
FALLOFF = 0.16
TWO_ROOT_PI = 1.1283791670955126
FACTOR = GRAVITY * FALLOFF**1.5


def pair_weight(dist_sq):
    square = dist_sq * FALLOFF
    inverse = lax.rsqrt(square)
    tail = 1.0 - lax.erf(square * inverse)
    bell = jnp.exp2(dist_sq * (-FALLOFF / math.log(2.0)))
    return (tail * inverse + bell * TWO_ROOT_PI) * (inverse * inverse)


def place():
    return lax.axis_index("sink"), lax.axis_index("src")


def greet(peers):
    barrier = pltpu.get_barrier_semaphore()
    for peer in peers:
        pl.semaphore_signal(
            barrier, inc=1, device_id=peer, device_id_type=pl.DeviceIdType.MESH
        )
    pl.semaphore_wait(barrier, len(peers))


def peers_of(chips, group):
    sink, src = place()
    core = lax.rem(sink, 2)
    half = sink // chips
    rings = sorted(range(chips // 2), key=lambda o: -min(o, chips // 2 - o))
    steps = [(h, o) for o in rings for h in (1, 0) if (h, o) != (0, 0)]
    rows = sorted(range(group), key=lambda o: -min(o, group - o))
    return sink, src, core, half, steps, rows


def moved(sink, chips, step, back=False):
    half, ring = step
    ring = chips // 2 - ring if back else ring
    within = lax.rem(lax.rem(sink, chips) // 2 + ring, chips // 2)
    return lax.rem(sink // chips + half, 2) * chips + within * 2 + lax.rem(sink, 2)


def remote(source, target, send, recv, device):
    return pltpu.make_async_remote_copy(
        src_ref=source,
        dst_ref=target,
        send_sem=send,
        recv_sem=recv,
        device_id=device,
        device_id_type=pl.DeviceIdType.MESH,
    )


def gather_kernel(
    chips, group, pos, mass, ids, count, column_out, rows_out, ids_out,
    pack, column_send, column_recv, row_send, row_recv, pass_send, pass_recv,
    hand_send, hand_recv, own_send, own_recv,
):
    sink, src, core, half, steps, rows = peers_of(chips, group)
    other = 1 - core
    across = lax.rem(sink + chips, 2 * chips)
    partner = (sink + 1 - 2 * core, src)
    diagonal = (across + 1 - 2 * core, src)
    column = [(moved(sink, chips, step), src) for step in steps]
    row = [
        (h, o, (across if h else sink, lax.rem(src + o, group)))
        for o in rows for h in (1, 0) if (h, o) != (0, 0)
    ]
    greet(column + [peer for h, o, peer in row if o] + [partner, diagonal])
    pack[0:24, :] = pos[...].reshape(24, CELLS)
    pack[24:32, :] = mass[...]
    mine = core * 2 + half
    ids_out[mine, 0:2, :] = ids[0, 0, :, 0:128]
    ids_out[mine, 2:4, :] = ids[0, 0, :, 128:256]
    ids_out[mine, 4:8, :] = jnp.full((4, 128), count[0, 0], jnp.int32)

    sends = []

    def start(copy):
        copy.start()
        sends.append(copy)

    for i, peer in enumerate(column):
        start(remote(pack, column_out.at[sink], column_send.at[i], column_recv.at[i], peer))
    for i, (h, o, peer) in enumerate(row):
        start(remote(pack, rows_out.at[mine, src], row_send.at[i], row_recv.at[i], peer))
    start(remote(pack, column_out.at[sink], own_send.at[0], own_recv.at[0], partner))
    start(remote(pack, rows_out.at[mine, src], own_send.at[1], own_recv.at[1], partner))
    pool = [partner, (across, src), diagonal]
    for i, peer in enumerate(pool):
        start(remote(ids_out.at[mine], ids_out.at[mine], own_send.at[2 + i], own_recv.at[2 + i], peer))
    column_out[sink] = pack[...]
    rows_out[mine, src] = pack[...]

    for i, (h, o, peer) in reversed(list(enumerate(row))):
        block = rows_out.at[core * 2 + lax.rem(half + h, 2), lax.rem(src + group - o, group)]
        remote(pack, block, row_send.at[i], row_recv.at[i], partner).wait_recv()
        start(remote(block, block, hand_send.at[i], hand_recv.at[i], partner))
    for i, step in reversed(list(enumerate(steps))):
        block = column_out.at[moved(sink, chips, step, back=True)]
        remote(pack, block, column_send.at[i], column_recv.at[i], partner).wait_recv()
        start(remote(block, block, pass_send.at[i], pass_recv.at[i], partner))

    for i, (h, o, peer) in reversed(list(enumerate(row))):
        block = rows_out.at[other * 2 + lax.rem(half + h, 2), lax.rem(src + group - o, group)]
        remote(pack, block, hand_send.at[i], hand_recv.at[i], partner).wait_recv()
    for i, step in reversed(list(enumerate(steps))):
        block = column_out.at[moved(partner[0], chips, step, back=True)]
        remote(pack, block, pass_send.at[i], pass_recv.at[i], partner).wait_recv()
    remote(pack, column_out.at[partner[0]], own_send.at[0], own_recv.at[0], partner).wait_recv()
    remote(pack, rows_out.at[other * 2 + half, src], own_send.at[1], own_recv.at[1], partner).wait_recv()
    origins = [other * 2 + half, core * 2 + 1 - half, other * 2 + 1 - half]
    for i, origin in enumerate(origins):
        remote(ids_out.at[mine], ids_out.at[origin], own_send.at[2 + i], own_recv.at[2 + i], partner).wait_recv()
    for copy in sends:
        copy.wait_send()


def pair_kernel(chips, group, ids, rows, column, row_force, column_force, parts, choose, acc, first_x, second_x):
    sink = lax.axis_index("sink")
    mine = lax.rem(sink, 2) * 2 + sink // chips
    counts = [ids[w, 4, 0] for w in range(4)]
    starts = [0]
    for w in range(4):
        starts.append(starts[w] + counts[w])
    every = starts[4]
    begin = mine * every // 4
    end = (mine + 1) * every // 4
    last = jnp.maximum(end - 1, 0)
    column_force[...] = jnp.zeros_like(column_force)

    for w in range(4):

        @pl.when((starts[w] < end) & (starts[w + 1] > begin))
        def _(w=w):
            for h in range(group):
                block = rows[w, h]
                high = block.astype(BF16).astype(F32)
                rest = block - high
                middle = rest.astype(BF16).astype(F32)
                low = rest - middle
                stacked = jnp.concatenate([high, middle, low, jnp.zeros_like(high)], axis=0)
                parts[w * group + h] = stacked.T.astype(BF16)

    depth = lax.broadcasted_iota(jnp.int32, (128, 512), 0)
    field = lax.broadcasted_iota(jnp.int32, (128, 512), 1) // 128
    hit = (depth < 96) & (depth % 32 // 8 == field)
    for k in range(8):
        choose[k] = jnp.where(hit & (depth % 8 == k), 1.0, 0.0).astype(BF16)
    acc[...] = jnp.zeros_like(acc)
    lane = lax.broadcasted_iota(jnp.int32, (8, 128), 1)

    def look(slot):
        slot = jnp.minimum(slot, last)
        which = sum(jnp.where(slot >= starts[w], 1, 0) for w in range(1, 4))
        p = slot
        for w in range(3):
            p = p - jnp.where(slot >= starts[w + 1], counts[w], 0)
        a = ids[which, p // 128 * 2, p % 128]
        b = ids[which, p // 128 * 2 + 1, p % 128]
        sink_block = which * group + a // LEAF_DEV % group
        return sink_block, a % LEAF_DEV, b // (LEAF_DEV * group), b % LEAF_DEV

    def fill(target, first):
        for u in range(UNROLL):
            sink_block, k, _, _ = look(first + u)
            target[u] = jnp.dot(parts[sink_block], choose[k], preferred_element_type=F32)

    def use(spread, first):
        done = []
        for u in range(UNROLL):
            sink_block, k, source_block, source_k = look(first + u)
            live = jnp.where(first + u < end, FACTOR, 0.0)
            at = sink_block % 4 * 32 + k
            here = [
                jnp.broadcast_to(column[source_block, pl.ds(8 * c + source_k, 1), :], (8, 128))
                for c in range(4)
            ]
            mass = here[3] * live
            masks = [lane == at + 8 * c for c in range(3)]
            source_sum = [jnp.zeros((8, 128), F32) for _ in range(3)]
            sink_sum = []
            for i in range(0, CELLS, 8):
                there = [spread[u, i : i + 8, 128 * c : 128 * c + 128] for c in range(4)]
                offset = [here[c] - there[c] for c in range(3)]
                dist_sq = (offset[0] * offset[0] + offset[1] * offset[1]) + (
                    offset[2] * offset[2] + SOFTEN
                )
                weight = (pair_weight(dist_sq) * there[3]) * mass
                force = [weight * offset[c] for c in range(3)]
                source_sum = [source_sum[c] + force[c] for c in range(3)]
                total = [jnp.sum(force[c], axis=1, keepdims=True) for c in range(3)]
                sink_sum.append(
                    jnp.where(
                        masks[0],
                        total[0],
                        jnp.where(masks[1], total[1], jnp.where(masks[2], total[2], 0.0)),
                    )
                )
            done.append((sink_block // 4, source_block, source_k, source_sum, sink_sum))
        for g, source_block, source_k, source_sum, sink_sum in done:
            for i, value in enumerate(sink_sum):
                acc[g, pl.ds(8 * i, 8), :] += value
            slot = source_block % 2 * chips + source_block // 2
            for c in range(3):
                column_force[slot, pl.ds(8 * c + source_k, 1), :] -= jnp.sum(
                    source_sum[c], axis=0, keepdims=True
                )

    fill(first_x, begin)

    def turn(i, carry):
        first = begin + i * (2 * UNROLL)
        fill(second_x, first + UNROLL)
        use(first_x, first)
        fill(first_x, first + 2 * UNROLL)
        use(second_x, first + UNROLL)
        return carry

    lax.fori_loop(0, (end - begin + 2 * UNROLL - 1) // (2 * UNROLL), turn, 0)
    for w in range(4):
        used = (starts[w] < end) & (starts[w + 1] > begin)

        @pl.when(used)
        def _(w=w):
            for g in range(group // 4):
                turned = acc[w * (group // 4) + g].T
                for h in range(4):
                    row_force[w, g * 4 + h] = turned[32 * h : 32 * h + FORCES, :]

        @pl.when(jnp.logical_not(used))
        def _(w=w):
            row_force[w] = jnp.zeros_like(row_force[w])


def reduce_kernel(
    chips, group, row_force, column_force, out,
    row_sum, column_sum, row_in, column_in, swap_row, swap_column,
    column_send, column_recv, row_send, row_recv, swap_send, swap_recv,
):
    sink, src, core, half, steps, rows = peers_of(chips, group)
    other = 1 - core
    across = lax.rem(sink + chips, 2 * chips)
    partner = (sink + 1 - 2 * core, src)
    column = [(moved(sink, chips, step), src) for step in steps]
    row = [
        (h, o, (across if h else sink, lax.rem(src + o, group)))
        for o in rows for h in (1, 0) if (h, o) != (0, 0)
    ]
    greet(column + [peer for h, o, peer in row if o] + [partner])
    to_column = remote(
        column_force.at[pl.ds(other * chips, chips)], swap_column,
        swap_send.at[0], swap_recv.at[0], partner,
    )
    to_row = remote(
        row_force.at[pl.ds(other * 2, 2)], swap_row, swap_send.at[1], swap_recv.at[1], partner
    )
    to_column.start()
    to_row.start()
    to_column.wait_recv()
    column_sum[...] = column_force[pl.ds(core * chips, chips)] + swap_column[...]
    sends = [to_column, to_row]
    for i, peer in enumerate(column):
        copy = remote(
            column_sum.at[peer[0] // 2], column_in.at[i], column_send.at[i], column_recv.at[i], peer
        )
        copy.start()
        sends.append(copy)
    to_row.wait_recv()
    row_sum[...] = row_force[pl.ds(core * 2, 2)] + swap_row[...]
    for i, (h, o, peer) in enumerate(row):
        copy = remote(
            row_sum.at[lax.rem(half + h, 2), peer[1]], row_in.at[i],
            row_send.at[i], row_recv.at[i], peer,
        )
        copy.start()
        sends.append(copy)
    total = column_sum[sink // 2] + row_sum[half, src]
    for i in reversed(range(len(row))):
        remote(row_sum.at[0, 0], row_in.at[i], row_send.at[i], row_recv.at[i], partner).wait_recv()
        total = total + row_in[i]
    for i in reversed(range(len(column))):
        remote(column_sum.at[0], column_in.at[i], column_send.at[i], column_recv.at[i], partner).wait_recv()
        total = total + column_in[i]
    out[...] = total.reshape(3, LEAF_DEV, CELLS)
    for copy in sends:
        copy.wait_send()


def per_device(chips, group, leaf_pos, leaf_mass, pair_ids, pair_count):
    vmem = pl.BlockSpec(memory_space=pltpu.VMEM)
    smem = pl.BlockSpec(memory_space=pltpu.SMEM)
    dma = pltpu.SemaphoreType.DMA
    column, rows, ids = pl.pallas_call(
        functools.partial(gather_kernel, chips, group),
        name="gather",
        out_shape=(
            jax.ShapeDtypeStruct((2 * chips, FIELDS, CELLS), F32),
            jax.ShapeDtypeStruct((4, group, FIELDS, CELLS), F32),
            jax.ShapeDtypeStruct((4, 8, CELLS), jnp.int32),
        ),
        in_specs=[vmem, vmem, vmem, smem],
        out_specs=(vmem, vmem, vmem),
        scratch_shapes=[
            pltpu.VMEM((FIELDS, CELLS), F32),
            dma((chips - 1,)), dma((chips - 1,)),
            dma((2 * group - 1,)), dma((2 * group - 1,)),
            dma((chips - 1,)), dma((chips - 1,)),
            dma((2 * group - 1,)), dma((2 * group - 1,)),
            dma((5,)), dma((5,)),
        ],
        compiler_params=pltpu.CompilerParams(
            collective_id=0, has_side_effects=True, vmem_limit_bytes=16 << 20
        ),
    )(jnp.transpose(leaf_pos, (1, 0, 2)), leaf_mass, pair_ids, pair_count)
    blocks = 4 * group
    row_force, column_force = pl.pallas_call(
        functools.partial(pair_kernel, chips, group),
        name="pairs",
        out_shape=(
            jax.ShapeDtypeStruct((4, group, FORCES, CELLS), F32),
            jax.ShapeDtypeStruct((2 * chips, FORCES, CELLS), F32),
        ),
        in_specs=[smem, vmem, vmem],
        out_specs=(vmem, vmem),
        scratch_shapes=[
            pltpu.VMEM((blocks, 128, 128), BF16),
            pltpu.VMEM((8, 128, 512), BF16),
            pltpu.VMEM((blocks // 4, 128, 128), F32),
            pltpu.VMEM((UNROLL, 128, 512), F32),
            pltpu.VMEM((UNROLL, 128, 512), F32),
        ],
        compiler_params=pltpu.CompilerParams(vmem_limit_bytes=40 << 20),
    )(ids, rows, column)
    force = pl.pallas_call(
        functools.partial(reduce_kernel, chips, group),
        name="reduce",
        out_shape=jax.ShapeDtypeStruct((3, LEAF_DEV, CELLS), F32),
        in_specs=[vmem, vmem],
        out_specs=vmem,
        scratch_shapes=[
            pltpu.VMEM((2, group, FORCES, CELLS), F32),
            pltpu.VMEM((chips, FORCES, CELLS), F32),
            pltpu.VMEM((2 * group - 1, FORCES, CELLS), F32),
            pltpu.VMEM((chips - 1, FORCES, CELLS), F32),
            pltpu.VMEM((2, group, FORCES, CELLS), F32),
            pltpu.VMEM((chips, FORCES, CELLS), F32),
            dma((chips - 1,)), dma((chips - 1,)),
            dma((2 * group - 1,)), dma((2 * group - 1,)),
            dma((2,)), dma((2,)),
        ],
        compiler_params=pltpu.CompilerParams(
            collective_id=1, has_side_effects=True, vmem_limit_bytes=16 << 20
        ),
    )(row_force, column_force)
    return jnp.transpose(force, (1, 0, 2))


def solution(mesh):
    return jax.shard_map(
        functools.partial(per_device, mesh.shape["sink"] // 2, mesh.shape["src"]),
        mesh=mesh,
        in_specs=(
            P(("sink", "src"), None, None),
            P(("sink", "src"), None),
            P("sink", "src", None, None),
            P("sink", "src"),
        ),
        out_specs=P(("sink", "src"), None, None),
        check_vma=False,
    )
```

```python
import functools
import math

import jax
import jax.numpy as jnp
from jax import lax
from jax.experimental import pallas as pl
from jax.experimental.pallas import tpu as pltpu
from jax.sharding import PartitionSpec as P

F32 = jnp.float32
BF16 = jnp.bfloat16
SOFTEN = 0.09
LEAF_DEV = 8
CELLS = 128
PAIR_CAP = 256
FIELDS = 32
FORCES = 24
UNROLL = 4
GRAVITY = 0.05
FALLOFF = 0.16
TWO_ROOT_PI = 1.1283791670955126
FACTOR = GRAVITY * FALLOFF**1.5


def pair_weight(dist_sq):
    square = dist_sq * FALLOFF
    inverse = lax.rsqrt(square)
    tail = 1.0 - lax.erf(square * inverse)
    bell = jnp.exp2(dist_sq * (-FALLOFF / math.log(2.0)))
    return (tail * inverse + bell * TWO_ROOT_PI) * (inverse * inverse)


def place():
    return lax.axis_index("sink"), lax.axis_index("src")


def greet(peers):
    barrier = pltpu.get_barrier_semaphore()
    for peer in peers:
        pl.semaphore_signal(
            barrier, inc=1, device_id=peer, device_id_type=pl.DeviceIdType.MESH
        )
    pl.semaphore_wait(barrier, len(peers))


def peers_of(chips, group):
    sink, src = place()
    core = lax.rem(sink, 2)
    half = sink // chips
    rings = sorted(range(chips // 2), key=lambda o: -min(o, chips // 2 - o))
    steps = [(h, o) for o in rings for h in (1, 0) if (h, o) != (0, 0)]
    rows = sorted(range(group), key=lambda o: -min(o, group - o))
    return sink, src, core, half, steps, rows


def moved(sink, chips, step, back=False):
    half, ring = step
    ring = chips // 2 - ring if back else ring
    within = lax.rem(lax.rem(sink, chips) // 2 + ring, chips // 2)
    return lax.rem(sink // chips + half, 2) * chips + within * 2 + lax.rem(sink, 2)


def remote(source, target, send, recv, device):
    return pltpu.make_async_remote_copy(
        src_ref=source,
        dst_ref=target,
        send_sem=send,
        recv_sem=recv,
        device_id=device,
        device_id_type=pl.DeviceIdType.MESH,
    )


def gather_kernel(
    chips, group, pos, mass, ids, count, column_out, ids_out, parts, choose,
    rows_out, pack, ids_in, load, column_send, column_recv, row_send, row_recv, pass_send, pass_recv,
    hand_send, hand_recv, own_send, own_recv,
):
    sink, src, core, half, steps, rows = peers_of(chips, group)
    other = 1 - core
    across = lax.rem(sink + chips, 2 * chips)
    partner = (sink + 1 - 2 * core, src)
    diagonal = (across + 1 - 2 * core, src)
    column = [(moved(sink, chips, step), src) for step in steps]
    row = [
        (h, o, (across if h else sink, lax.rem(src + o, group)))
        for o in rows for h in (1, 0) if (h, o) != (0, 0)
    ]
    loads = [
        pltpu.make_async_copy(source, target, load.at[i])
        for i, (source, target) in enumerate((
            (pos, pack.at[0:3]), (mass, pack.at[3]), (ids, ids_in),
        ))
    ]
    for copy in loads:
        copy.start()
    greet(column + [peer for h, o, peer in row if o] + [partner, diagonal])
    for copy in loads:
        copy.wait()
    mine = core * 2 + half
    ids_out[mine, 0:2, :] = ids_in[0, 0, :, 0:128]
    ids_out[mine, 2:4, :] = ids_in[0, 0, :, 128:256]
    ids_out[mine, 4:8, :] = jnp.full((4, CELLS), count[0, 0], jnp.int32)

    sends = []

    def start(copy):
        copy.start()
        sends.append(copy)

    for i, peer in enumerate(column):
        start(remote(pack, column_out.at[sink], column_send.at[i], column_recv.at[i], peer))
    for i, (h, o, peer) in enumerate(row):
        start(remote(pack, rows_out.at[mine, src], row_send.at[i], row_recv.at[i], peer))
    start(remote(pack, column_out.at[sink], own_send.at[0], own_recv.at[0], partner))
    start(remote(pack, rows_out.at[mine, src], own_send.at[1], own_recv.at[1], partner))
    pool = [partner, (across, src), diagonal]
    for i, peer in enumerate(pool):
        start(remote(ids_out.at[mine], ids_out.at[mine], own_send.at[2 + i], own_recv.at[2 + i], peer))
    column_out[sink] = pack[...]
    rows_out[mine, src] = pack[...]

    depth = lax.broadcasted_iota(jnp.int32, (128, 512), 0)
    field = lax.broadcasted_iota(jnp.int32, (128, 512), 1) // 128
    hit = (depth < 96) & (depth % 32 // 8 == field)
    for k in range(8):
        choose[k] = jnp.where(hit & (depth % 8 == k), 1.0, 0.0).astype(BF16)

    def split(line, at):
        block = rows_out[line, at].reshape(FIELDS, CELLS)
        high = block.astype(BF16).astype(F32)
        rest = block - high
        middle = rest.astype(BF16).astype(F32)
        low = rest - middle
        stacked = jnp.concatenate([high, middle, low, jnp.zeros_like(high)], axis=0)
        parts[line, at] = stacked.T.astype(BF16)

    for i, (h, o, peer) in reversed(list(enumerate(row))):
        block = rows_out.at[core * 2 + lax.rem(half + h, 2), lax.rem(src + group - o, group)]
        remote(pack, block, row_send.at[i], row_recv.at[i], partner).wait_recv()
        start(remote(block, block, hand_send.at[i], hand_recv.at[i], partner))
    for i, step in reversed(list(enumerate(steps))):
        block = column_out.at[moved(sink, chips, step, back=True)]
        remote(pack, block, column_send.at[i], column_recv.at[i], partner).wait_recv()
        start(remote(block, block, pass_send.at[i], pass_recv.at[i], partner))
        split(core * 2 + i // group, i % group)
    split(core * 2 + 1, group - 1)

    for i, (h, o, peer) in reversed(list(enumerate(row))):
        block = rows_out.at[other * 2 + lax.rem(half + h, 2), lax.rem(src + group - o, group)]
        remote(pack, block, hand_send.at[i], hand_recv.at[i], partner).wait_recv()
    remote(pack, rows_out.at[other * 2 + half, src], own_send.at[1], own_recv.at[1], partner).wait_recv()
    for i in range(2 * group):
        split(other * 2 + i // group, i % group)
    for i, step in reversed(list(enumerate(steps))):
        block = column_out.at[moved(partner[0], chips, step, back=True)]
        remote(pack, block, pass_send.at[i], pass_recv.at[i], partner).wait_recv()
    remote(pack, column_out.at[partner[0]], own_send.at[0], own_recv.at[0], partner).wait_recv()
    origins = [other * 2 + half, core * 2 + 1 - half, other * 2 + 1 - half]
    for i, origin in enumerate(origins):
        remote(ids_out.at[mine], ids_out.at[origin], own_send.at[2 + i], own_recv.at[2 + i], partner).wait_recv()
    for copy in sends:
        copy.wait_send()


def pair_kernel(
    chips, group, ids, parts, choose, column, row_force, column_force, acc, first_x, second_x
):
    sink = lax.axis_index("sink")
    mine = lax.rem(sink, 2) * 2 + sink // chips
    counts = [ids[w, 4, 0] for w in range(4)]
    starts = [0]
    for w in range(4):
        starts.append(starts[w] + counts[w])
    every = starts[4]
    begin = mine * every // 4
    end = (mine + 1) * every // 4
    last = jnp.maximum(end - 1, 0)
    column_force[...] = jnp.zeros_like(column_force)

    acc[...] = jnp.zeros_like(acc)
    lane = lax.broadcasted_iota(jnp.int32, (8, 128), 1)

    def look(slot):
        slot = jnp.minimum(slot, last)
        which = sum(jnp.where(slot >= starts[w], 1, 0) for w in range(1, 4))
        p = slot
        for w in range(3):
            p = p - jnp.where(slot >= starts[w + 1], counts[w], 0)
        a = ids[which, p // 128 * 2, p % 128]
        b = ids[which, p // 128 * 2 + 1, p % 128]
        sink_block = which * group + a // LEAF_DEV % group
        return sink_block, a % LEAF_DEV, b // (LEAF_DEV * group), b % LEAF_DEV

    def fill(target, first):
        for u in range(UNROLL):
            sink_block, k, _, _ = look(first + u)
            target[u] = jnp.dot(parts[sink_block // group, sink_block % group], choose[k], preferred_element_type=F32)

    def use(spread, first):
        done = []
        for u in range(UNROLL):
            sink_block, k, source_block, source_k = look(first + u)
            live = jnp.where(first + u < end, FACTOR, 0.0)
            at = sink_block % 4 * 32 + k
            here = [
                jnp.broadcast_to(column[source_block, c, pl.ds(source_k, 1), :], (8, 128))
                for c in range(4)
            ]
            mass = here[3] * live
            masks = [lane == at + 8 * c for c in range(3)]
            source_sum = [jnp.zeros((8, 128), F32) for _ in range(3)]
            sink_sum = []
            for i in range(0, CELLS, 8):
                there = [spread[u, i : i + 8, 128 * c : 128 * c + 128] for c in range(4)]
                offset = [here[c] - there[c] for c in range(3)]
                dist_sq = (offset[0] * offset[0] + offset[1] * offset[1]) + (
                    offset[2] * offset[2] + SOFTEN
                )
                weight = (pair_weight(dist_sq) * there[3]) * mass
                force = [weight * offset[c] for c in range(3)]
                source_sum = [source_sum[c] + force[c] for c in range(3)]
                total = [jnp.sum(force[c], axis=1, keepdims=True) for c in range(3)]
                sink_sum.append(
                    jnp.where(
                        masks[0],
                        total[0],
                        jnp.where(masks[1], total[1], jnp.where(masks[2], total[2], 0.0)),
                    )
                )
            done.append((sink_block // 4, source_block, source_k, source_sum, sink_sum))
        for g, source_block, source_k, source_sum, sink_sum in done:
            for i, value in enumerate(sink_sum):
                acc[g, pl.ds(8 * i, 8), :] += value
            slot = source_block % 2 * chips + source_block // 2
            for c in range(3):
                column_force[slot, pl.ds(8 * c + source_k, 1), :] -= jnp.sum(
                    source_sum[c], axis=0, keepdims=True
                )

    fill(first_x, begin)

    def turn(i, carry):
        first = begin + i * (2 * UNROLL)
        fill(second_x, first + UNROLL)
        use(first_x, first)
        fill(first_x, first + 2 * UNROLL)
        use(second_x, first + UNROLL)
        return carry

    lax.fori_loop(0, (end - begin + 2 * UNROLL - 1) // (2 * UNROLL), turn, 0)
    for w in range(4):
        used = (starts[w] < end) & (starts[w + 1] > begin)

        @pl.when(used)
        def _(w=w):
            for g in range(group // 4):
                turned = acc[w * (group // 4) + g].T
                for h in range(4):
                    row_force[w, g * 4 + h] = turned[32 * h : 32 * h + FORCES, :]

        @pl.when(jnp.logical_not(used))
        def _(w=w):
            row_force[w] = jnp.zeros_like(row_force[w])


def reduce_kernel(
    chips, group, row_force, column_force, out,
    row_sum, column_sum, row_in, column_in, swap_row, swap_column,
    column_send, column_recv, row_send, row_recv, swap_send, swap_recv,
):
    sink, src, core, half, steps, rows = peers_of(chips, group)
    other = 1 - core
    across = lax.rem(sink + chips, 2 * chips)
    partner = (sink + 1 - 2 * core, src)
    column = [(moved(sink, chips, step), src) for step in steps]
    row = [
        (h, o, (across if h else sink, lax.rem(src + o, group)))
        for o in rows for h in (1, 0) if (h, o) != (0, 0)
    ]
    greet(column + [peer for h, o, peer in row if o] + [partner])
    to_column = remote(
        column_force.at[pl.ds(other * chips, chips)], swap_column,
        swap_send.at[0], swap_recv.at[0], partner,
    )
    to_row = remote(
        row_force.at[pl.ds(other * 2, 2)], swap_row, swap_send.at[1], swap_recv.at[1], partner
    )
    to_column.start()
    to_row.start()
    to_column.wait_recv()
    column_sum[...] = column_force[pl.ds(core * chips, chips)] + swap_column[...]
    sends = [to_column, to_row]
    for i, peer in enumerate(column):
        copy = remote(
            column_sum.at[peer[0] // 2], column_in.at[i], column_send.at[i], column_recv.at[i], peer
        )
        copy.start()
        sends.append(copy)
    to_row.wait_recv()
    row_sum[...] = row_force[pl.ds(core * 2, 2)] + swap_row[...]
    for i, (h, o, peer) in enumerate(row):
        copy = remote(
            row_sum.at[lax.rem(half + h, 2), peer[1]], row_in.at[i],
            row_send.at[i], row_recv.at[i], peer,
        )
        copy.start()
        sends.append(copy)
    total = column_sum[sink // 2] + row_sum[half, src]
    for i in reversed(range(len(row))):
        remote(row_sum.at[0, 0], row_in.at[i], row_send.at[i], row_recv.at[i], partner).wait_recv()
        total = total + row_in[i]
    for i in reversed(range(len(column))):
        remote(column_sum.at[0], column_in.at[i], column_send.at[i], column_recv.at[i], partner).wait_recv()
        total = total + column_in[i]
    out[...] = total.reshape(3, LEAF_DEV, CELLS)
    for copy in sends:
        copy.wait_send()


def per_device(chips, group, leaf_pos, leaf_mass, pair_ids, pair_count):
    vmem = pl.BlockSpec(memory_space=pltpu.VMEM)
    smem = pl.BlockSpec(memory_space=pltpu.SMEM)
    hbm = pl.BlockSpec(memory_space=pltpu.HBM)
    dma = pltpu.SemaphoreType.DMA
    column, ids, parts, choose = pl.pallas_call(
        functools.partial(gather_kernel, chips, group),
        name="gather",
        out_shape=(
            jax.ShapeDtypeStruct((2 * chips, 4, LEAF_DEV, CELLS), F32),
            jax.ShapeDtypeStruct((4, 8, CELLS), jnp.int32),
            jax.ShapeDtypeStruct((4, group, 128, 128), BF16),
            jax.ShapeDtypeStruct((8, 128, 512), BF16),
        ),
        in_specs=[hbm] * 3 + [smem],
        out_specs=(vmem,) * 4,
        scratch_shapes=[
            pltpu.VMEM((4, group, 4, LEAF_DEV, CELLS), F32),
            pltpu.VMEM((4, LEAF_DEV, CELLS), F32),
            pltpu.VMEM((1, 1, 2, PAIR_CAP), jnp.int32),
            dma((3,)),
            dma((chips - 1,)), dma((chips - 1,)),
            dma((2 * group - 1,)), dma((2 * group - 1,)),
            dma((chips - 1,)), dma((chips - 1,)),
            dma((2 * group - 1,)), dma((2 * group - 1,)),
            dma((5,)), dma((5,)),
        ],
        compiler_params=pltpu.CompilerParams(
            collective_id=0, has_side_effects=True, vmem_limit_bytes=16 << 20
        ),
    )(*(
        pltpu.with_memory_space_constraint(x, pltpu.HBM)
        for x in (jnp.transpose(leaf_pos, (1, 0, 2)), leaf_mass, pair_ids)
    ), pair_count)
    blocks = 4 * group
    row_force, column_force = pl.pallas_call(
        functools.partial(pair_kernel, chips, group),
        name="pairs",
        out_shape=(
            jax.ShapeDtypeStruct((4, group, FORCES, CELLS), F32),
            jax.ShapeDtypeStruct((2 * chips, FORCES, CELLS), F32),
        ),
        in_specs=[smem, vmem, vmem, vmem],
        out_specs=(vmem, vmem),
        scratch_shapes=[
            pltpu.VMEM((blocks // 4, 128, 128), F32),
            pltpu.VMEM((UNROLL, 128, 512), F32),
            pltpu.VMEM((UNROLL, 128, 512), F32),
        ],
        compiler_params=pltpu.CompilerParams(vmem_limit_bytes=40 << 20),
    )(ids, parts, choose, column)
    force = pl.pallas_call(
        functools.partial(reduce_kernel, chips, group),
        name="reduce",
        out_shape=jax.ShapeDtypeStruct((3, LEAF_DEV, CELLS), F32),
        in_specs=[vmem, vmem],
        out_specs=vmem,
        scratch_shapes=[
            pltpu.VMEM((2, group, FORCES, CELLS), F32),
            pltpu.VMEM((chips, FORCES, CELLS), F32),
            pltpu.VMEM((2 * group - 1, FORCES, CELLS), F32),
            pltpu.VMEM((chips - 1, FORCES, CELLS), F32),
            pltpu.VMEM((2, group, FORCES, CELLS), F32),
            pltpu.VMEM((chips, FORCES, CELLS), F32),
            dma((chips - 1,)), dma((chips - 1,)),
            dma((2 * group - 1,)), dma((2 * group - 1,)),
            dma((2,)), dma((2,)),
        ],
        compiler_params=pltpu.CompilerParams(
            collective_id=1, has_side_effects=True, vmem_limit_bytes=16 << 20
        ),
    )(row_force, column_force)
    return jnp.transpose(force, (1, 0, 2))


def solution(mesh):
    return jax.shard_map(
        functools.partial(per_device, mesh.shape["sink"] // 2, mesh.shape["src"]),
        mesh=mesh,
        in_specs=(
            P(("sink", "src"), None, None),
            P(("sink", "src"), None),
            P("sink", "src", None, None),
            P("sink", "src"),
        ),
        out_specs=P(("sink", "src"), None, None),
        check_vma=False,
    )
```

```python
import functools
import math

import jax
import jax.numpy as jnp
from jax import lax
from jax.experimental import pallas as pl
from jax.experimental.pallas import tpu as pltpu
from jax.sharding import PartitionSpec as P

F32 = jnp.float32
BF16 = jnp.bfloat16
SOFTEN = 0.09
LEAF_DEV = 8
CELLS = 128
PAIR_CAP = 256
FIELDS = 32
FORCES = 24
UNROLL = 4
GRAVITY = 0.05
FALLOFF = 0.16
TWO_ROOT_PI = 1.1283791670955126
FACTOR = GRAVITY * FALLOFF**1.5


def pair_weight(dist_sq):
    square = dist_sq * FALLOFF
    inverse = lax.rsqrt(square)
    tail = 1.0 - lax.erf(square * inverse)
    bell = jnp.exp2(dist_sq * (-FALLOFF / math.log(2.0)))
    return (tail * inverse + bell * TWO_ROOT_PI) * (inverse * inverse)


def place():
    return lax.axis_index("sink"), lax.axis_index("src")


def greet(peers):
    barrier = pltpu.get_barrier_semaphore()
    for peer in peers:
        pl.semaphore_signal(
            barrier, inc=1, device_id=peer, device_id_type=pl.DeviceIdType.MESH
        )
    pl.semaphore_wait(barrier, len(peers))


def peers_of(chips, group):
    sink, src = place()
    core = lax.rem(sink, 2)
    half = sink // chips
    rings = sorted(range(chips // 2), key=lambda o: -min(o, chips // 2 - o))
    steps = [(h, o) for o in rings for h in (1, 0) if (h, o) != (0, 0)]
    rows = sorted(range(group), key=lambda o: -min(o, group - o))
    return sink, src, core, half, steps, rows


def moved(sink, chips, step, back=False):
    half, ring = step
    ring = chips // 2 - ring if back else ring
    within = lax.rem(lax.rem(sink, chips) // 2 + ring, chips // 2)
    return lax.rem(sink // chips + half, 2) * chips + within * 2 + lax.rem(sink, 2)


def place_of(sink, chips):
    return lax.rem(sink, 2) * chips + sink // 2


def remote(source, target, send, recv, device):
    return pltpu.make_async_remote_copy(
        src_ref=source,
        dst_ref=target,
        send_sem=send,
        recv_sem=recv,
        device_id=device,
        device_id_type=pl.DeviceIdType.MESH,
    )


def gather_kernel(
    chips, group, pos, mass, ids, count, column_out, codes, rows_out,
    ids_out, pack, ids_in, load, column_send, column_recv, row_send, row_recv, pass_send, pass_recv,
    hand_send, hand_recv, own_send, own_recv,
):
    sink, src, core, half, steps, rows = peers_of(chips, group)
    other = 1 - core
    across = lax.rem(sink + chips, 2 * chips)
    partner = (sink + 1 - 2 * core, src)
    diagonal = (across + 1 - 2 * core, src)
    column = [(moved(sink, chips, step), src) for step in steps]
    row = [
        (h, o, (across if h else sink, lax.rem(src + o, group)))
        for o in rows for h in (1, 0) if (h, o) != (0, 0)
    ]
    loads = [
        pltpu.make_async_copy(source, target, load.at[i])
        for i, (source, target) in enumerate((
            (pos, pack.at[0:3]), (mass, pack.at[3]), (ids, ids_in),
        ))
    ]
    for copy in loads:
        copy.start()
    greet(column + [peer for h, o, peer in row if o] + [partner, diagonal])
    for copy in loads:
        copy.wait()
    mine = core * 2 + half
    ids_out[mine, 0:2, :] = ids_in[0, 0, :, 0:128]
    ids_out[mine, 2:4, :] = ids_in[0, 0, :, 128:256]
    ids_out[mine, 4:8, :] = jnp.full((4, CELLS), count[0, 0], jnp.int32)

    sends = []

    def start(copy):
        copy.start()
        sends.append(copy)

    for i, peer in enumerate(column):
        start(remote(pack, column_out.at[place_of(sink, chips)], column_send.at[i], column_recv.at[i], peer))
    for i, (h, o, peer) in enumerate(row):
        start(remote(pack, rows_out.at[mine, src], row_send.at[i], row_recv.at[i], peer))
    start(remote(pack, column_out.at[place_of(sink, chips)], own_send.at[0], own_recv.at[0], partner))
    start(remote(pack, rows_out.at[mine, src], own_send.at[1], own_recv.at[1], partner))
    pool = [partner, (across, src), diagonal]
    for i, peer in enumerate(pool):
        start(remote(ids_out.at[mine], ids_out.at[mine], own_send.at[2 + i], own_recv.at[2 + i], peer))
    column_out[place_of(sink, chips)] = pack[...]
    rows_out[mine, src] = pack[...]

    for i, (h, o, peer) in reversed(list(enumerate(row))):
        block = rows_out.at[core * 2 + lax.rem(half + h, 2), lax.rem(src + group - o, group)]
        remote(pack, block, row_send.at[i], row_recv.at[i], partner).wait_recv()
        start(remote(block, block, hand_send.at[i], hand_recv.at[i], partner))
    for i, step in reversed(list(enumerate(steps))):
        block = column_out.at[place_of(moved(sink, chips, step, back=True), chips)]
        remote(pack, block, column_send.at[i], column_recv.at[i], partner).wait_recv()
        start(remote(block, block, pass_send.at[i], pass_recv.at[i], partner))

    for i, (h, o, peer) in reversed(list(enumerate(row))):
        block = rows_out.at[other * 2 + lax.rem(half + h, 2), lax.rem(src + group - o, group)]
        remote(pack, block, hand_send.at[i], hand_recv.at[i], partner).wait_recv()
    remote(pack, rows_out.at[other * 2 + half, src], own_send.at[1], own_recv.at[1], partner).wait_recv()
    for i, step in reversed(list(enumerate(steps))):
        block = column_out.at[place_of(moved(partner[0], chips, step, back=True), chips)]
        remote(pack, block, pass_send.at[i], pass_recv.at[i], partner).wait_recv()
    remote(pack, column_out.at[place_of(partner[0], chips)], own_send.at[0], own_recv.at[0], partner).wait_recv()
    origins = [other * 2 + half, core * 2 + 1 - half, other * 2 + 1 - half]
    for i, origin in enumerate(origins):
        remote(ids_out.at[mine], ids_out.at[origin], own_send.at[2 + i], own_recv.at[2 + i], partner).wait_recv()
    for w in range(4):
        for h in range(2):
            a = ids_out[w, 2 * h : 2 * h + 1, :]
            b = ids_out[w, 2 * h + 1 : 2 * h + 2, :]
            owner = b // (LEAF_DEV * group)
            source = (owner % 2 * chips + owner // 2) * LEAF_DEV + b % LEAF_DEV
            target = w * group * LEAF_DEV + a % (group * LEAF_DEV)
            codes[2 * w + h : 2 * w + h + 1, :] = target * 256 + source
        codes[8 + w : 9 + w, :] = ids_out[w, 4:5, :]
    for copy in sends:
        copy.wait_send()


def pair_kernel(
    chips, group, ids, rows_out, column, row_force, column_force, parts, choose, acc, first_x, second_x
):
    sink = lax.axis_index("sink")
    mine = lax.rem(sink, 2) * 2 + sink // chips
    starts = [0]
    for w in range(4):
        starts.append(starts[w] + ids[8 + w, 0])
    every = starts[4]
    begin = mine * every // 4
    end = (mine + 1) * every // 4
    last = jnp.maximum(end - 1, 0)
    column_force[...] = jnp.zeros_like(column_force)
    depth = lax.broadcasted_iota(jnp.int32, (128, 512), 0)
    field = lax.broadcasted_iota(jnp.int32, (128, 512), 1) // 128
    hit = (depth < 96) & (depth % 32 // 8 == field)
    for k in range(8):
        choose[k] = jnp.where(hit & (depth % 8 == k), 1.0, 0.0).astype(BF16)

    def split(line, at):
        block = rows_out[line, at].reshape(FIELDS, CELLS)
        high = block.astype(BF16).astype(F32)
        rest = block - high
        middle = rest.astype(BF16).astype(F32)
        low = rest - middle
        stacked = jnp.concatenate([high, middle, low, jnp.zeros_like(high)], axis=0)
        parts[line * group + at] = stacked.T.astype(BF16)

    for w in range(4):

        @pl.when((starts[w] < end) & (starts[w + 1] > begin))
        def _(w=w):
            for h in range(group):
                split(w, h)


    acc[...] = jnp.zeros_like(acc)
    lane = lax.broadcasted_iota(jnp.int32, (8, 128), 1)

    def look(slot):
        slot = jnp.minimum(slot, last)
        shift = 0
        for w in range(1, 4):
            shift = jnp.where(slot >= starts[w], w * PAIR_CAP - starts[w], shift)
        slot = slot + shift
        return ids[slot >> 7, slot & 127]

    def fill(target, first):
        for u in range(UNROLL):
            code = look(first + u)
            target[u] = jnp.dot(parts[code >> 11], choose[code >> 8 & 7], preferred_element_type=F32)

    def use(spread, first):
        done = []
        for u in range(UNROLL):
            code = look(first + u)
            source_block = code >> 3 & 31
            source_k = code & 7
            live = jnp.where(first + u < end, FACTOR, 0.0)
            at = (code >> 11 & 3) * 32 + (code >> 8 & 7)
            here = [
                jnp.broadcast_to(column[source_block, c, pl.ds(source_k, 1), :], (8, 128))
                for c in range(4)
            ]
            mass = here[3] * live
            masks = [lane == at + 8 * c for c in range(3)]
            source_sum = [jnp.zeros((8, 128), F32) for _ in range(3)]
            sink_sum = []
            for i in range(0, CELLS, 8):
                there = [spread[u, i : i + 8, 128 * c : 128 * c + 128] for c in range(4)]
                offset = [here[c] - there[c] for c in range(3)]
                dist_sq = (offset[0] * offset[0] + offset[1] * offset[1]) + (
                    offset[2] * offset[2] + SOFTEN
                )
                weight = (pair_weight(dist_sq) * there[3]) * mass
                force = [weight * offset[c] for c in range(3)]
                source_sum = [source_sum[c] + force[c] for c in range(3)]
                total = [jnp.sum(force[c], axis=1, keepdims=True) for c in range(3)]
                sink_sum.append(
                    jnp.where(
                        masks[0],
                        total[0],
                        jnp.where(masks[1], total[1], jnp.where(masks[2], total[2], 0.0)),
                    )
                )
            done.append((code >> 13, source_block, source_k, source_sum, sink_sum))
        for g, source_block, source_k, source_sum, sink_sum in done:
            for i, value in enumerate(sink_sum):
                acc[g, pl.ds(8 * i, 8), :] += value
            for c in range(3):
                column_force[source_block, pl.ds(8 * c + source_k, 1), :] -= jnp.sum(
                    source_sum[c], axis=0, keepdims=True
                )

    fill(first_x, begin)

    def turn(i, carry):
        first = begin + i * (2 * UNROLL)
        fill(second_x, first + UNROLL)
        use(first_x, first)
        fill(first_x, first + 2 * UNROLL)
        use(second_x, first + UNROLL)
        return carry

    lax.fori_loop(0, (end - begin + 2 * UNROLL - 1) // (2 * UNROLL), turn, 0)
    for w in range(4):
        used = (starts[w] < end) & (starts[w + 1] > begin)

        @pl.when(used)
        def _(w=w):
            for g in range(group // 4):
                turned = acc[w * (group // 4) + g].T
                for h in range(4):
                    row_force[w, g * 4 + h] = turned[32 * h : 32 * h + FORCES, :]

        @pl.when(jnp.logical_not(used))
        def _(w=w):
            row_force[w] = jnp.zeros_like(row_force[w])


def reduce_kernel(
    chips, group, row_force, column_force, out,
    row_sum, column_sum, row_in, column_in, swap_row, swap_column,
    column_send, column_recv, row_send, row_recv, swap_send, swap_recv,
):
    sink, src, core, half, steps, rows = peers_of(chips, group)
    other = 1 - core
    across = lax.rem(sink + chips, 2 * chips)
    partner = (sink + 1 - 2 * core, src)
    column = [(moved(sink, chips, step), src) for step in steps]
    row = [
        (h, o, (across if h else sink, lax.rem(src + o, group)))
        for o in rows for h in (1, 0) if (h, o) != (0, 0)
    ]
    greet(column + [peer for h, o, peer in row if o] + [partner])
    to_column = remote(
        column_force.at[pl.ds(other * chips, chips)], swap_column,
        swap_send.at[0], swap_recv.at[0], partner,
    )
    to_row = remote(
        row_force.at[pl.ds(other * 2, 2)], swap_row, swap_send.at[1], swap_recv.at[1], partner
    )
    to_column.start()
    to_row.start()
    to_column.wait_recv()
    column_sum[...] = column_force[pl.ds(core * chips, chips)] + swap_column[...]
    sends = [to_column, to_row]
    for i, peer in enumerate(column):
        copy = remote(
            column_sum.at[peer[0] // 2], column_in.at[i], column_send.at[i], column_recv.at[i], peer
        )
        copy.start()
        sends.append(copy)
    to_row.wait_recv()
    row_sum[...] = row_force[pl.ds(core * 2, 2)] + swap_row[...]
    for i, (h, o, peer) in enumerate(row):
        copy = remote(
            row_sum.at[lax.rem(half + h, 2), peer[1]], row_in.at[i],
            row_send.at[i], row_recv.at[i], peer,
        )
        copy.start()
        sends.append(copy)
    total = column_sum[sink // 2] + row_sum[half, src]
    for i in reversed(range(len(row))):
        remote(row_sum.at[0, 0], row_in.at[i], row_send.at[i], row_recv.at[i], partner).wait_recv()
        total = total + row_in[i]
    for i in reversed(range(len(column))):
        remote(column_sum.at[0], column_in.at[i], column_send.at[i], column_recv.at[i], partner).wait_recv()
        total = total + column_in[i]
    out[...] = total.reshape(3, LEAF_DEV, CELLS)
    for copy in sends:
        copy.wait_send()


def per_device(chips, group, leaf_pos, leaf_mass, pair_ids, pair_count):
    vmem = pl.BlockSpec(memory_space=pltpu.VMEM)
    smem = pl.BlockSpec(memory_space=pltpu.SMEM)
    hbm = pl.BlockSpec(memory_space=pltpu.HBM)
    dma = pltpu.SemaphoreType.DMA
    column, codes, rows = pl.pallas_call(
        functools.partial(gather_kernel, chips, group),
        name="gather",
        out_shape=(
            jax.ShapeDtypeStruct((2 * chips, 4, LEAF_DEV, CELLS), F32),
            jax.ShapeDtypeStruct((16, CELLS), jnp.int32),
            jax.ShapeDtypeStruct((4, group, 4, LEAF_DEV, CELLS), F32),
        ),
        in_specs=[hbm] * 3 + [smem],
        out_specs=(vmem,) * 3,
        scratch_shapes=[
            pltpu.VMEM((4, 8, CELLS), jnp.int32),
            pltpu.VMEM((4, LEAF_DEV, CELLS), F32),
            pltpu.VMEM((1, 1, 2, PAIR_CAP), jnp.int32),
            dma((3,)),
            dma((chips - 1,)), dma((chips - 1,)),
            dma((2 * group - 1,)), dma((2 * group - 1,)),
            dma((chips - 1,)), dma((chips - 1,)),
            dma((2 * group - 1,)), dma((2 * group - 1,)),
            dma((5,)), dma((5,)),
        ],
        compiler_params=pltpu.CompilerParams(
            collective_id=0, has_side_effects=True, vmem_limit_bytes=16 << 20
        ),
    )(*(
        pltpu.with_memory_space_constraint(x, pltpu.HBM)
        for x in (jnp.transpose(leaf_pos, (1, 0, 2)), leaf_mass, pair_ids)
    ), pair_count)
    blocks = 4 * group
    row_force, column_force = pl.pallas_call(
        functools.partial(pair_kernel, chips, group),
        name="pairs",
        out_shape=(
            jax.ShapeDtypeStruct((4, group, FORCES, CELLS), F32),
            jax.ShapeDtypeStruct((2 * chips, FORCES, CELLS), F32),
        ),
        in_specs=[smem, vmem, vmem],
        out_specs=(vmem, vmem),
        scratch_shapes=[
            pltpu.VMEM((4 * group, 128, 128), BF16),
            pltpu.VMEM((8, 128, 512), BF16),
            pltpu.VMEM((blocks // 4, 128, 128), F32),
            pltpu.VMEM((UNROLL, 128, 512), F32),
            pltpu.VMEM((UNROLL, 128, 512), F32),
        ],
        compiler_params=pltpu.CompilerParams(vmem_limit_bytes=40 << 20),
    )(codes, rows, column)
    force = pl.pallas_call(
        functools.partial(reduce_kernel, chips, group),
        name="reduce",
        out_shape=jax.ShapeDtypeStruct((3, LEAF_DEV, CELLS), F32),
        in_specs=[vmem, vmem],
        out_specs=vmem,
        scratch_shapes=[
            pltpu.VMEM((2, group, FORCES, CELLS), F32),
            pltpu.VMEM((chips, FORCES, CELLS), F32),
            pltpu.VMEM((2 * group - 1, FORCES, CELLS), F32),
            pltpu.VMEM((chips - 1, FORCES, CELLS), F32),
            pltpu.VMEM((2, group, FORCES, CELLS), F32),
            pltpu.VMEM((chips, FORCES, CELLS), F32),
            dma((chips - 1,)), dma((chips - 1,)),
            dma((2 * group - 1,)), dma((2 * group - 1,)),
            dma((2,)), dma((2,)),
        ],
        compiler_params=pltpu.CompilerParams(
            collective_id=1, has_side_effects=True, vmem_limit_bytes=16 << 20
        ),
    )(row_force, column_force)
    return jnp.transpose(force, (1, 0, 2))


def solution(mesh):
    return jax.shard_map(
        functools.partial(per_device, mesh.shape["sink"] // 2, mesh.shape["src"]),
        mesh=mesh,
        in_specs=(
            P(("sink", "src"), None, None),
            P(("sink", "src"), None),
            P("sink", "src", None, None),
            P("sink", "src"),
        ),
        out_specs=P(("sink", "src"), None, None),
        check_vma=False,
    )
```

```python
import functools
import math

import jax
import jax.numpy as jnp
from jax import lax
from jax.experimental import pallas as pl
from jax.experimental.pallas import tpu as pltpu
from jax.sharding import PartitionSpec as P

F32 = jnp.float32
BF16 = jnp.bfloat16
SOFTEN = 0.09
LEAF_DEV = 8
CELLS = 128
PAIR_CAP = 256
FIELDS = 32
FORCES = 24
UNROLL = 4
GRAVITY = 0.05
FALLOFF = 0.16
TWO_ROOT_PI = 1.1283791670955126
FACTOR = GRAVITY * FALLOFF**1.5


def pair_weight(dist_sq):
    square = dist_sq * FALLOFF
    inverse = lax.rsqrt(square)
    tail = 1.0 - lax.erf(square * inverse)
    bell = jnp.exp2(dist_sq * (-FALLOFF / math.log(2.0)))
    return (tail * inverse + bell * TWO_ROOT_PI) * (inverse * inverse)


def place():
    return lax.axis_index("sink"), lax.axis_index("src")


def greet(peers, meanwhile):
    barrier = pltpu.get_barrier_semaphore()
    for peer in peers:
        pl.semaphore_signal(
            barrier, inc=1, device_id=peer, device_id_type=pl.DeviceIdType.MESH
        )
    meanwhile()
    pl.semaphore_wait(barrier, len(peers))


def peers_of(chips, group):
    sink, src = place()
    core = lax.rem(sink, 2)
    half = sink // chips
    rings = sorted(range(chips // 2), key=lambda o: -min(o, chips // 2 - o))
    steps = [(h, o) for o in rings for h in (1, 0) if (h, o) != (0, 0)]
    rows = sorted(range(group), key=lambda o: -min(o, group - o))
    return sink, src, core, half, steps, rows


def moved(sink, chips, step, back=False):
    half, ring = step
    ring = chips // 2 - ring if back else ring
    within = lax.rem(lax.rem(sink, chips) // 2 + ring, chips // 2)
    return lax.rem(sink // chips + half, 2) * chips + within * 2 + lax.rem(sink, 2)


def remote(source, target, send, recv, device):
    return pltpu.make_async_remote_copy(
        src_ref=source,
        dst_ref=target,
        send_sem=send,
        recv_sem=recv,
        device_id=device,
        device_id_type=pl.DeviceIdType.MESH,
    )


def compact(group, core, ids, w):
    a = jnp.concatenate([ids[w, 0:1, :], ids[w, 2:3, :]], axis=1)
    b = jnp.concatenate([ids[w, 1:2, :], ids[w, 3:4, :]], axis=1)
    count = jnp.concatenate([ids[w, 4:5, :], ids[w, 5:6, :]], axis=1)
    owner = b // (LEAF_DEV * group)
    slot = lax.broadcasted_iota(jnp.int32, (1, PAIR_CAP), 1)
    chosen = (slot < count) & (owner % 2 == core)
    flag = jnp.where(chosen, 1.0, 0.0)
    sink = (w * group * LEAF_DEV + a % (group * LEAF_DEV)).astype(F32)
    source = (owner // 2 * LEAF_DEV + b % LEAF_DEV).astype(F32)
    row = lax.broadcasted_iota(jnp.int32, (PAIR_CAP, PAIR_CAP), 0)
    lane = lax.broadcasted_iota(jnp.int32, (PAIR_CAP, PAIR_CAP), 1)
    before = jnp.where(row < lane, 1.0, 0.0).astype(BF16)
    flags = jnp.broadcast_to(flag, (16, PAIR_CAP)).astype(BF16)
    order = jnp.dot(flags, before, preferred_element_type=F32)[0:1, :]
    order = jnp.where(chosen, order, -1.0)
    pick = jnp.where(row.astype(F32) == order, 1.0, 0.0).astype(BF16)
    values = jnp.concatenate(
        [jnp.broadcast_to(sink, (8, PAIR_CAP)), jnp.broadcast_to(source, (8, PAIR_CAP))], axis=0
    ).astype(BF16)
    packed = lax.dot_general(
        values, pick, (((1,), (1,)), ((), ())), preferred_element_type=F32
    ).astype(jnp.int32)
    total = jnp.sum(flag, axis=1, keepdims=True).astype(jnp.int32)
    return packed[0:1, :] * 128 + packed[8:9, :], total


def gather_kernel(
    chips, group, pos, mass, ids, count, column_out, codes, rows_out,
    ids_out, pack, ids_in, load, column_send, column_recv, row_send, row_recv,
    hand_send, hand_recv, own_send, own_recv,
):
    sink, src, core, half, steps, rows = peers_of(chips, group)
    other = 1 - core
    across = lax.rem(sink + chips, 2 * chips)
    partner = (sink + 1 - 2 * core, src)
    diagonal = (across + 1 - 2 * core, src)
    column = [(moved(sink, chips, step), src) for step in steps]
    row = [
        (h, o, (across if h else sink, lax.rem(src + o, group)))
        for o in rows for h in (1, 0) if (h, o) != (0, 0)
    ]
    loads = [
        pltpu.make_async_copy(source, target, load.at[i])
        for i, (source, target) in enumerate((
            (pos, pack.at[0:3]), (mass, pack.at[3]), (ids, ids_in),
        ))
    ]
    for copy in loads:
        copy.start()
    mine = core * 2 + half

    def own_block():
        for copy in loads:
            copy.wait()
        ids_out[mine, 0:2, :] = ids_in[0, 0, :, 0:128]
        ids_out[mine, 2:4, :] = ids_in[0, 0, :, 128:256]
        ids_out[mine, 4:8, :] = jnp.full((4, CELLS), count[0, 0], jnp.int32)
        column_out[sink // 2] = pack[...]
        rows_out[mine, src] = pack[...]

    greet(column + [peer for h, o, peer in row if o] + [partner, diagonal], own_block)

    sends = []

    def start(copy):
        copy.start()
        sends.append(copy)

    for i, peer in enumerate(column):
        start(remote(pack, column_out.at[sink // 2], column_send.at[i], column_recv.at[i], peer))
    for i, (h, o, peer) in enumerate(row):
        start(remote(pack, rows_out.at[mine, src], row_send.at[i], row_recv.at[i], peer))
    start(remote(pack, rows_out.at[mine, src], own_send.at[0], own_recv.at[0], partner))
    pool = [partner, (across, src), diagonal]
    for i, peer in enumerate(pool):
        start(remote(ids_out.at[mine], ids_out.at[mine], own_send.at[1 + i], own_recv.at[1 + i], peer))

    for i, (h, o, peer) in reversed(list(enumerate(row))):
        block = rows_out.at[core * 2 + lax.rem(half + h, 2), lax.rem(src + group - o, group)]
        remote(pack, block, row_send.at[i], row_recv.at[i], partner).wait_recv()
        start(remote(block, block, hand_send.at[i], hand_recv.at[i], partner))

    origins = [other * 2 + half, core * 2 + 1 - half, other * 2 + 1 - half]
    for i, origin in enumerate(origins):
        remote(ids_out.at[mine], ids_out.at[origin], own_send.at[1 + i], own_recv.at[1 + i], partner).wait_recv()
    for w in range(4):
        code, total = compact(group, core, ids_out, w)
        codes[2 * w : 2 * w + 1, :] = code[:, 0:128]
        codes[2 * w + 1 : 2 * w + 2, :] = code[:, 128:256]
        codes[8 + w : 9 + w, :] = jnp.broadcast_to(total, (1, CELLS))
    codes[12:16, :] = jnp.zeros((4, CELLS), jnp.int32)

    for i, step in reversed(list(enumerate(steps))):
        block = column_out.at[moved(sink, chips, step, back=True) // 2]
        remote(pack, block, column_send.at[i], column_recv.at[i], partner).wait_recv()
    remote(pack, rows_out.at[other * 2 + half, src], own_send.at[0], own_recv.at[0], partner).wait_recv()
    for i, (h, o, peer) in reversed(list(enumerate(row))):
        block = rows_out.at[other * 2 + lax.rem(half + h, 2), lax.rem(src + group - o, group)]
        remote(pack, block, hand_send.at[i], hand_recv.at[i], partner).wait_recv()
    for copy in sends:
        copy.wait_send()


def pair_kernel(
    chips, group, ids, rows_out, column, acc, column_force, parts, choose, first_x, second_x
):
    sink = lax.axis_index("sink")
    half = sink // chips
    starts = [0]
    for w in range(4):
        starts.append(starts[w] + ids[8 + w, 0])
    every = starts[4]
    begin = half * every // 2
    end = (half + 1) * every // 2
    last = jnp.maximum(end - 1, 0)
    column_force[...] = jnp.zeros_like(column_force)
    depth = lax.broadcasted_iota(jnp.int32, (128, 512), 0)
    field = lax.broadcasted_iota(jnp.int32, (128, 512), 1) // 128
    hit = (depth < 96) & (depth % 32 // 8 == field)
    for k in range(8):
        choose[k] = jnp.where(hit & (depth % 8 == k), 1.0, 0.0).astype(BF16)

    def split(line, at):
        block = rows_out[line, at].reshape(FIELDS, CELLS)
        high = block.astype(BF16).astype(F32)
        rest = block - high
        middle = rest.astype(BF16).astype(F32)
        low = rest - middle
        stacked = jnp.concatenate([high, middle, low, jnp.zeros_like(high)], axis=0)
        parts[line * group + at] = stacked.T.astype(BF16)

    for w in range(4):

        @pl.when((starts[w] < end) & (starts[w + 1] > begin))
        def _(w=w):
            for h in range(group):
                split(w, h)

    acc[...] = jnp.zeros_like(acc)
    lane = lax.broadcasted_iota(jnp.int32, (8, 128), 1)

    def look(slot):
        slot = jnp.minimum(slot, last)
        shift = 0
        for w in range(1, 4):
            shift = jnp.where(slot >= starts[w], w * PAIR_CAP - starts[w], shift)
        slot = slot + shift
        return ids[slot >> 7, slot & 127]

    def fill(target, first):
        for u in range(UNROLL):
            code = look(first + u)
            target[u] = jnp.dot(parts[code >> 10], choose[code >> 7 & 7], preferred_element_type=F32)

    def use(spread, first):
        done = []
        for u in range(UNROLL):
            code = look(first + u)
            source_block = code >> 3 & 15
            source_k = code & 7
            live = jnp.where(first + u < end, FACTOR, 0.0)
            at = (code >> 10 & 3) * 32 + (code >> 7 & 7)
            here = [
                jnp.broadcast_to(column[source_block, c, pl.ds(source_k, 1), :], (8, 128))
                for c in range(4)
            ]
            mass = here[3] * live
            masks = [lane == at + 8 * c for c in range(3)]
            source_sum = [jnp.zeros((8, 128), F32) for _ in range(3)]
            sink_sum = []
            for i in range(0, CELLS, 8):
                there = [spread[u, i : i + 8, 128 * c : 128 * c + 128] for c in range(4)]
                offset = [here[c] - there[c] for c in range(3)]
                dist_sq = (offset[0] * offset[0] + offset[1] * offset[1]) + (
                    offset[2] * offset[2] + SOFTEN
                )
                weight = (pair_weight(dist_sq) * there[3]) * mass
                force = [weight * offset[c] for c in range(3)]
                source_sum = [source_sum[c] + force[c] for c in range(3)]
                total = [jnp.sum(force[c], axis=1, keepdims=True) for c in range(3)]
                sink_sum.append(
                    jnp.where(
                        masks[0],
                        total[0],
                        jnp.where(masks[1], total[1], jnp.where(masks[2], total[2], 0.0)),
                    )
                )
            done.append((code >> 12, source_block, source_k, source_sum, sink_sum))
        for g, source_block, source_k, source_sum, sink_sum in done:
            for i, value in enumerate(sink_sum):
                acc[g, pl.ds(8 * i, 8), :] += value
            for c in range(3):
                column_force[source_block, pl.ds(8 * c + source_k, 1), :] -= jnp.sum(
                    source_sum[c], axis=0, keepdims=True
                )

    fill(first_x, begin)

    def turn(i, carry):
        first = begin + i * (2 * UNROLL)
        fill(second_x, first + UNROLL)
        use(first_x, first)
        fill(first_x, first + 2 * UNROLL)
        use(second_x, first + UNROLL)
        return carry

    lax.fori_loop(0, (end - begin + 2 * UNROLL - 1) // (2 * UNROLL), turn, 0)


def reduce_kernel(
    chips, group, acc, column_force, out,
    row_force, row_sum, row_in, column_in, swap_row,
    column_send, column_recv, row_send, row_recv, swap_send, swap_recv,
):
    sink, src, core, half, steps, rows = peers_of(chips, group)
    other = 1 - core
    across = lax.rem(sink + chips, 2 * chips)
    partner = (sink + 1 - 2 * core, src)
    column = [(moved(sink, chips, step), src) for step in steps]
    row = [
        (h, o, (across if h else sink, lax.rem(src + o, group)))
        for o in rows for h in (1, 0) if (h, o) != (0, 0)
    ]

    def turn_rows():
        for g in range(group):
            turned = acc[g].T
            for h in range(4):
                at = g * 4 + h
                row_force[at // group, at % group] = turned[32 * h : 32 * h + FORCES, :]

    greet(column + [peer for h, o, peer in row if o] + [partner], turn_rows)
    to_row = remote(
        row_force.at[pl.ds(other * 2, 2)], swap_row, swap_send.at[0], swap_recv.at[0], partner
    )
    to_row.start()
    sends = [to_row]
    for i, peer in enumerate(column):
        copy = remote(
            column_force.at[peer[0] // 2], column_in.at[i], column_send.at[i], column_recv.at[i], peer
        )
        copy.start()
        sends.append(copy)
    to_row.wait_recv()
    row_sum[...] = row_force[pl.ds(core * 2, 2)] + swap_row[...]
    for i, (h, o, peer) in enumerate(row):
        copy = remote(
            row_sum.at[lax.rem(half + h, 2), peer[1]], row_in.at[i],
            row_send.at[i], row_recv.at[i], peer,
        )
        copy.start()
        sends.append(copy)
    total = column_force[sink // 2] + row_sum[half, src]
    for i in reversed(range(len(row))):
        remote(row_sum.at[0, 0], row_in.at[i], row_send.at[i], row_recv.at[i], partner).wait_recv()
        total = total + row_in[i]
    for i in reversed(range(len(column))):
        remote(column_force.at[0], column_in.at[i], column_send.at[i], column_recv.at[i], partner).wait_recv()
        total = total + column_in[i]
    out[...] = total.reshape(3, LEAF_DEV, CELLS)
    for copy in sends:
        copy.wait_send()


def per_device(chips, group, leaf_pos, leaf_mass, pair_ids, pair_count):
    vmem = pl.BlockSpec(memory_space=pltpu.VMEM)
    smem = pl.BlockSpec(memory_space=pltpu.SMEM)
    hbm = pl.BlockSpec(memory_space=pltpu.HBM)
    dma = pltpu.SemaphoreType.DMA
    column, codes, rows = pl.pallas_call(
        functools.partial(gather_kernel, chips, group),
        name="gather",
        out_shape=(
            jax.ShapeDtypeStruct((chips, 4, LEAF_DEV, CELLS), F32),
            jax.ShapeDtypeStruct((16, CELLS), jnp.int32),
            jax.ShapeDtypeStruct((4, group, 4, LEAF_DEV, CELLS), F32),
        ),
        in_specs=[hbm] * 3 + [smem],
        out_specs=(vmem,) * 3,
        scratch_shapes=[
            pltpu.VMEM((4, 8, CELLS), jnp.int32),
            pltpu.VMEM((4, LEAF_DEV, CELLS), F32),
            pltpu.VMEM((1, 1, 2, PAIR_CAP), jnp.int32),
            dma((3,)),
            dma((chips - 1,)), dma((chips - 1,)),
            dma((2 * group - 1,)), dma((2 * group - 1,)),
            dma((2 * group - 1,)), dma((2 * group - 1,)),
            dma((4,)), dma((4,)),
        ],
        compiler_params=pltpu.CompilerParams(
            collective_id=0, has_side_effects=True, vmem_limit_bytes=16 << 20
        ),
    )(*(
        pltpu.with_memory_space_constraint(x, pltpu.HBM)
        for x in (jnp.transpose(leaf_pos, (1, 0, 2)), leaf_mass, pair_ids)
    ), pair_count)
    blocks = 4 * group
    acc, column_force = pl.pallas_call(
        functools.partial(pair_kernel, chips, group),
        name="pairs",
        out_shape=(
            jax.ShapeDtypeStruct((blocks // 4, 128, 128), F32),
            jax.ShapeDtypeStruct((chips, FORCES, CELLS), F32),
        ),
        in_specs=[smem, vmem, vmem],
        out_specs=(vmem, vmem),
        scratch_shapes=[
            pltpu.VMEM((4 * group, 128, 128), BF16),
            pltpu.VMEM((8, 128, 512), BF16),
            pltpu.VMEM((UNROLL, 128, 512), F32),
            pltpu.VMEM((UNROLL, 128, 512), F32),
        ],
        compiler_params=pltpu.CompilerParams(vmem_limit_bytes=40 << 20),
    )(codes, rows, column)
    force = pl.pallas_call(
        functools.partial(reduce_kernel, chips, group),
        name="reduce",
        out_shape=jax.ShapeDtypeStruct((3, LEAF_DEV, CELLS), F32),
        in_specs=[vmem, vmem],
        out_specs=vmem,
        scratch_shapes=[
            pltpu.VMEM((4, group, FORCES, CELLS), F32),
            pltpu.VMEM((2, group, FORCES, CELLS), F32),
            pltpu.VMEM((2 * group - 1, FORCES, CELLS), F32),
            pltpu.VMEM((chips - 1, FORCES, CELLS), F32),
            pltpu.VMEM((2, group, FORCES, CELLS), F32),
            dma((chips - 1,)), dma((chips - 1,)),
            dma((2 * group - 1,)), dma((2 * group - 1,)),
            dma((1,)), dma((1,)),
        ],
        compiler_params=pltpu.CompilerParams(
            collective_id=1, has_side_effects=True, vmem_limit_bytes=16 << 20
        ),
    )(acc, column_force)
    return jnp.transpose(force, (1, 0, 2))


def solution(mesh):
    return jax.shard_map(
        functools.partial(per_device, mesh.shape["sink"] // 2, mesh.shape["src"]),
        mesh=mesh,
        in_specs=(
            P(("sink", "src"), None, None),
            P(("sink", "src"), None),
            P("sink", "src", None, None),
            P("sink", "src"),
        ),
        out_specs=P(("sink", "src"), None, None),
        check_vma=False,
    )
```

```python
import functools
import math

import jax
import jax.numpy as jnp
from jax import lax
from jax.experimental import pallas as pl
from jax.experimental.pallas import tpu as pltpu
from jax.sharding import PartitionSpec as P

F32 = jnp.float32
BF16 = jnp.bfloat16
SOFTEN = 0.09
LEAF_DEV = 8
CELLS = 128
PAIR_CAP = 256
FIELDS = 32
FORCES = 24
UNROLL = 4
GRAVITY = 0.05
FALLOFF = 0.16
TWO_ROOT_PI = 1.1283791670955126
FACTOR = GRAVITY * FALLOFF**1.5


def pair_weight(dist_sq):
    square = dist_sq * FALLOFF
    inverse = lax.rsqrt(square)
    tail = 1.0 - lax.erf(square * inverse)
    bell = jnp.exp2(dist_sq * (-FALLOFF / math.log(2.0)))
    return (tail * inverse + bell * TWO_ROOT_PI) * (inverse * inverse)


def place():
    return lax.axis_index("sink"), lax.axis_index("src")


def greet(peers, meanwhile):
    barrier = pltpu.get_barrier_semaphore()
    for peer in peers:
        pl.semaphore_signal(
            barrier, inc=1, device_id=peer, device_id_type=pl.DeviceIdType.MESH
        )
    meanwhile()
    pl.semaphore_wait(barrier, len(peers))


def peers_of(chips, group):
    sink, src = place()
    core = lax.rem(sink, 2)
    half = sink // chips
    steps = sorted(range(1, chips // 2), key=lambda o: -min(o, chips // 2 - o))
    rows = sorted(range(group), key=lambda o: -min(o, group - o))
    return sink, src, core, half, steps, rows


def ringed(sink, chips, step):
    return lax.rem(lax.rem(sink, chips) // 2 + step, chips // 2)


def moved(sink, chips, step):
    return sink // chips * chips + ringed(sink, chips, step) * 2 + lax.rem(sink, 2)


def remote(source, target, send, recv, device):
    return pltpu.make_async_remote_copy(
        src_ref=source,
        dst_ref=target,
        send_sem=send,
        recv_sem=recv,
        device_id=device,
        device_id_type=pl.DeviceIdType.MESH,
    )


def compact(chips, group, core, half, ids, w):
    a = jnp.concatenate([ids[w, 0:1, :], ids[w, 2:3, :]], axis=1)
    b = jnp.concatenate([ids[w, 1:2, :], ids[w, 3:4, :]], axis=1)
    count = jnp.concatenate([ids[w, 4:5, :], ids[w, 5:6, :]], axis=1)
    owner = b // (LEAF_DEV * group)
    slot = lax.broadcasted_iota(jnp.int32, (1, PAIR_CAP), 1)
    chosen = (slot < count) & (owner % 2 == core) & (owner // chips == half)
    flag = jnp.where(chosen, 1.0, 0.0)
    sink = (w * group * LEAF_DEV + a % (group * LEAF_DEV)).astype(F32)
    source = (owner % chips // 2 * LEAF_DEV + b % LEAF_DEV).astype(F32)
    row = lax.broadcasted_iota(jnp.int32, (PAIR_CAP, PAIR_CAP), 0)
    lane = lax.broadcasted_iota(jnp.int32, (PAIR_CAP, PAIR_CAP), 1)
    before = jnp.where(row < lane, 1.0, 0.0).astype(BF16)
    flags = jnp.broadcast_to(flag, (16, PAIR_CAP)).astype(BF16)
    order = jnp.dot(flags, before, preferred_element_type=F32)[0:1, :]
    order = jnp.where(chosen, order, -1.0)
    pick = jnp.where(row.astype(F32) == order, 1.0, 0.0).astype(BF16)
    values = jnp.concatenate(
        [jnp.broadcast_to(sink, (8, PAIR_CAP)), jnp.broadcast_to(source, (8, PAIR_CAP))], axis=0
    ).astype(BF16)
    packed = lax.dot_general(
        values, pick, (((1,), (1,)), ((), ())), preferred_element_type=F32
    ).astype(jnp.int32)
    total = jnp.sum(flag, axis=1, keepdims=True).astype(jnp.int32)
    return packed[0:1, :] * 64 + packed[8:9, :], total


def gather_kernel(
    chips, group, pos, mass, ids, count, column_out, codes, rows_out,
    ids_out, pack, ids_in, load, column_send, column_recv, row_send, row_recv,
    hand_send, hand_recv, own_send, own_recv,
):
    sink, src, core, half, steps, rows = peers_of(chips, group)
    other = 1 - core
    across = lax.rem(sink + chips, 2 * chips)
    partner = (sink + 1 - 2 * core, src)
    diagonal = (across + 1 - 2 * core, src)
    column = [(moved(sink, chips, step), src) for step in steps]
    row = [
        (h, o, (across if h else sink, lax.rem(src + o, group)))
        for o in rows for h in (1, 0) if (h, o) != (0, 0)
    ]
    loads = [
        pltpu.make_async_copy(source, target, load.at[i])
        for i, (source, target) in enumerate((
            (pos, pack.at[0:3]), (mass, pack.at[3]), (ids, ids_in),
        ))
    ]
    for copy in loads:
        copy.start()
    mine = core * 2 + half

    def own_block():
        for copy in loads:
            copy.wait()
        ids_out[mine, 0:2, :] = ids_in[0, 0, :, 0:128]
        ids_out[mine, 2:4, :] = ids_in[0, 0, :, 128:256]
        ids_out[mine, 4:8, :] = jnp.full((4, CELLS), count[0, 0], jnp.int32)
        column_out[ringed(sink, chips, 0)] = pack[...]
        rows_out[mine, src] = pack[...]

    greet(column + [peer for h, o, peer in row] + [partner, diagonal], own_block)

    sends = []

    def start(copy):
        copy.start()
        sends.append(copy)

    for i, peer in enumerate(column):
        start(remote(pack, column_out.at[ringed(sink, chips, 0)], column_send.at[i], column_recv.at[i], peer))
    for i, (h, o, peer) in enumerate(row):
        start(remote(pack, rows_out.at[mine, src], row_send.at[i], row_recv.at[i], peer))
    start(remote(pack, rows_out.at[mine, src], own_send.at[0], own_recv.at[0], partner))
    pool = [partner, (across, src), diagonal]
    for i, peer in enumerate(pool):
        start(remote(ids_out.at[mine], ids_out.at[mine], own_send.at[1 + i], own_recv.at[1 + i], peer))

    for i, (h, o, peer) in reversed(list(enumerate(row))):
        block = rows_out.at[core * 2 + lax.rem(half + h, 2), lax.rem(src + group - o, group)]
        remote(pack, block, row_send.at[i], row_recv.at[i], partner).wait_recv()
        start(remote(block, block, hand_send.at[i], hand_recv.at[i], partner))

    origins = [other * 2 + half, core * 2 + 1 - half, other * 2 + 1 - half]
    for i, origin in enumerate(origins):
        remote(ids_out.at[mine], ids_out.at[origin], own_send.at[1 + i], own_recv.at[1 + i], partner).wait_recv()
    for w in range(4):
        code, total = compact(chips, group, core, half, ids_out, w)
        codes[2 * w : 2 * w + 1, :] = code[:, 0:128]
        codes[2 * w + 1 : 2 * w + 2, :] = code[:, 128:256]
        codes[8 + w : 9 + w, :] = jnp.broadcast_to(total, (1, CELLS))
    codes[12:16, :] = jnp.zeros((4, CELLS), jnp.int32)

    for i, step in reversed(list(enumerate(steps))):
        block = column_out.at[ringed(sink, chips, chips // 2 - step)]
        remote(pack, block, column_send.at[i], column_recv.at[i], partner).wait_recv()
    remote(pack, rows_out.at[other * 2 + half, src], own_send.at[0], own_recv.at[0], partner).wait_recv()
    for i, (h, o, peer) in reversed(list(enumerate(row))):
        block = rows_out.at[other * 2 + lax.rem(half + h, 2), lax.rem(src + group - o, group)]
        remote(pack, block, hand_send.at[i], hand_recv.at[i], partner).wait_recv()
    for copy in sends:
        copy.wait_send()


def pair_kernel(
    chips, group, ids, rows_out, column, acc, column_force, parts, choose, first_x, second_x
):
    starts = [0]
    for w in range(4):
        starts.append(starts[w] + ids[8 + w, 0])
    every = starts[4]
    last = jnp.maximum(every - 1, 0)
    column_force[...] = jnp.zeros_like(column_force)
    depth = lax.broadcasted_iota(jnp.int32, (128, 512), 0)
    field = lax.broadcasted_iota(jnp.int32, (128, 512), 1) // 128
    hit = (depth < 96) & (depth % 32 // 8 == field)
    for k in range(8):
        choose[k] = jnp.where(hit & (depth % 8 == k), 1.0, 0.0).astype(BF16)

    def split(line, at):
        block = rows_out[line, at].reshape(FIELDS, CELLS)
        high = block.astype(BF16).astype(F32)
        rest = block - high
        middle = rest.astype(BF16).astype(F32)
        low = rest - middle
        stacked = jnp.concatenate([high, middle, low, jnp.zeros_like(high)], axis=0)
        parts[line * group + at] = stacked.T.astype(BF16)

    for w in range(4):

        @pl.when(starts[w] < starts[w + 1])
        def _(w=w):
            for h in range(group):
                split(w, h)

    acc[...] = jnp.zeros_like(acc)
    lane = lax.broadcasted_iota(jnp.int32, (8, 128), 1)

    def look(slot):
        slot = jnp.minimum(slot, last)
        shift = 0
        for w in range(1, 4):
            shift = jnp.where(slot >= starts[w], w * PAIR_CAP - starts[w], shift)
        slot = slot + shift
        return ids[slot >> 7, slot & 127]

    def fill(target, first):
        for u in range(UNROLL):
            code = look(first + u)
            target[u] = jnp.dot(parts[code >> 9], choose[code >> 6 & 7], preferred_element_type=F32)

    def use(spread, first):
        done = []
        for u in range(UNROLL):
            code = look(first + u)
            source_block = code >> 3 & 7
            source_k = code & 7
            live = jnp.where(first + u < every, FACTOR, 0.0)
            at = (code >> 9 & 3) * 32 + (code >> 6 & 7)
            here = [
                jnp.broadcast_to(column[source_block, c, pl.ds(source_k, 1), :], (8, 128))
                for c in range(4)
            ]
            mass = here[3] * live
            masks = [lane == at + 8 * c for c in range(3)]
            source_sum = [jnp.zeros((8, 128), F32) for _ in range(3)]
            sink_sum = []
            for i in range(0, CELLS, 8):
                there = [spread[u, i : i + 8, 128 * c : 128 * c + 128] for c in range(4)]
                offset = [here[c] - there[c] for c in range(3)]
                dist_sq = (offset[0] * offset[0] + offset[1] * offset[1]) + (
                    offset[2] * offset[2] + SOFTEN
                )
                weight = (pair_weight(dist_sq) * there[3]) * mass
                force = [weight * offset[c] for c in range(3)]
                source_sum = [source_sum[c] + force[c] for c in range(3)]
                total = [jnp.sum(force[c], axis=1, keepdims=True) for c in range(3)]
                sink_sum.append(
                    jnp.where(
                        masks[0],
                        total[0],
                        jnp.where(masks[1], total[1], jnp.where(masks[2], total[2], 0.0)),
                    )
                )
            done.append((code >> 11, source_block, source_k, source_sum, sink_sum))
        for g, source_block, source_k, source_sum, sink_sum in done:
            for i, value in enumerate(sink_sum):
                acc[g, pl.ds(8 * i, 8), :] += value
            for c in range(3):
                column_force[source_block, pl.ds(8 * c + source_k, 1), :] -= jnp.sum(
                    source_sum[c], axis=0, keepdims=True
                )

    fill(first_x, 0)

    def turn(i, carry):
        first = i * (2 * UNROLL)
        fill(second_x, first + UNROLL)
        use(first_x, first)
        fill(first_x, first + 2 * UNROLL)
        use(second_x, first + UNROLL)
        return carry

    lax.fori_loop(0, (every + 2 * UNROLL - 1) // (2 * UNROLL), turn, 0)


def reduce_kernel(
    chips, group, acc, column_force, out,
    row_force, row_sum, row_in, column_in, swap_row,
    column_send, column_recv, row_send, row_recv, swap_send, swap_recv,
):
    sink, src, core, half, steps, rows = peers_of(chips, group)
    other = 1 - core
    across = lax.rem(sink + chips, 2 * chips)
    partner = (sink + 1 - 2 * core, src)
    column = [(moved(sink, chips, step), src) for step in steps]
    row = [
        (h, o, (across if h else sink, lax.rem(src + o, group)))
        for o in rows for h in (1, 0) if (h, o) != (0, 0)
    ]

    def turn_rows():
        for g in range(group):
            turned = acc[g].T
            for h in range(4):
                at = g * 4 + h
                row_force[at // group, at % group] = turned[32 * h : 32 * h + FORCES, :]

    greet(column + [peer for h, o, peer in row] + [partner], turn_rows)
    to_row = remote(
        row_force.at[pl.ds(other * 2, 2)], swap_row, swap_send.at[0], swap_recv.at[0], partner
    )
    to_row.start()
    sends = [to_row]
    for i, peer in enumerate(column):
        copy = remote(
            column_force.at[ringed(sink, chips, steps[i])], column_in.at[i], column_send.at[i], column_recv.at[i], peer
        )
        copy.start()
        sends.append(copy)
    to_row.wait_recv()
    row_sum[...] = row_force[pl.ds(core * 2, 2)] + swap_row[...]
    for i, (h, o, peer) in enumerate(row):
        copy = remote(
            row_sum.at[lax.rem(half + h, 2), peer[1]], row_in.at[i],
            row_send.at[i], row_recv.at[i], peer,
        )
        copy.start()
        sends.append(copy)
    total = column_force[ringed(sink, chips, 0)] + row_sum[half, src]
    for i in reversed(range(len(row))):
        remote(row_sum.at[0, 0], row_in.at[i], row_send.at[i], row_recv.at[i], partner).wait_recv()
        total = total + row_in[i]
    for i in reversed(range(len(column))):
        remote(column_force.at[0], column_in.at[i], column_send.at[i], column_recv.at[i], partner).wait_recv()
        total = total + column_in[i]
    out[...] = total.reshape(3, LEAF_DEV, CELLS)
    for copy in sends:
        copy.wait_send()


def per_device(chips, group, leaf_pos, leaf_mass, pair_ids, pair_count):
    vmem = pl.BlockSpec(memory_space=pltpu.VMEM)
    smem = pl.BlockSpec(memory_space=pltpu.SMEM)
    hbm = pl.BlockSpec(memory_space=pltpu.HBM)
    dma = pltpu.SemaphoreType.DMA
    ring = chips // 2
    column, codes, rows = pl.pallas_call(
        functools.partial(gather_kernel, chips, group),
        name="gather",
        out_shape=(
            jax.ShapeDtypeStruct((ring, 4, LEAF_DEV, CELLS), F32),
            jax.ShapeDtypeStruct((16, CELLS), jnp.int32),
            jax.ShapeDtypeStruct((4, group, 4, LEAF_DEV, CELLS), F32),
        ),
        in_specs=[hbm] * 3 + [smem],
        out_specs=(vmem,) * 3,
        scratch_shapes=[
            pltpu.VMEM((4, 8, CELLS), jnp.int32),
            pltpu.VMEM((4, LEAF_DEV, CELLS), F32),
            pltpu.VMEM((1, 1, 2, PAIR_CAP), jnp.int32),
            dma((3,)),
            dma((ring - 1,)), dma((ring - 1,)),
            dma((2 * group - 1,)), dma((2 * group - 1,)),
            dma((2 * group - 1,)), dma((2 * group - 1,)),
            dma((4,)), dma((4,)),
        ],
        compiler_params=pltpu.CompilerParams(
            collective_id=0, has_side_effects=True, vmem_limit_bytes=16 << 20
        ),
    )(*(
        pltpu.with_memory_space_constraint(x, pltpu.HBM)
        for x in (jnp.transpose(leaf_pos, (1, 0, 2)), leaf_mass, pair_ids)
    ), pair_count)
    blocks = 4 * group
    acc, column_force = pl.pallas_call(
        functools.partial(pair_kernel, chips, group),
        name="pairs",
        out_shape=(
            jax.ShapeDtypeStruct((blocks // 4, 128, 128), F32),
            jax.ShapeDtypeStruct((ring, FORCES, CELLS), F32),
        ),
        in_specs=[smem, vmem, vmem],
        out_specs=(vmem, vmem),
        scratch_shapes=[
            pltpu.VMEM((4 * group, 128, 128), BF16),
            pltpu.VMEM((8, 128, 512), BF16),
            pltpu.VMEM((UNROLL, 128, 512), F32),
            pltpu.VMEM((UNROLL, 128, 512), F32),
        ],
        compiler_params=pltpu.CompilerParams(vmem_limit_bytes=40 << 20),
    )(codes, rows, column)
    force = pl.pallas_call(
        functools.partial(reduce_kernel, chips, group),
        name="reduce",
        out_shape=jax.ShapeDtypeStruct((3, LEAF_DEV, CELLS), F32),
        in_specs=[vmem, vmem],
        out_specs=vmem,
        scratch_shapes=[
            pltpu.VMEM((4, group, FORCES, CELLS), F32),
            pltpu.VMEM((2, group, FORCES, CELLS), F32),
            pltpu.VMEM((2 * group - 1, FORCES, CELLS), F32),
            pltpu.VMEM((ring - 1, FORCES, CELLS), F32),
            pltpu.VMEM((2, group, FORCES, CELLS), F32),
            dma((ring - 1,)), dma((ring - 1,)),
            dma((2 * group - 1,)), dma((2 * group - 1,)),
            dma((1,)), dma((1,)),
        ],
        compiler_params=pltpu.CompilerParams(
            collective_id=1, has_side_effects=True, vmem_limit_bytes=16 << 20
        ),
    )(acc, column_force)
    return jnp.transpose(force, (1, 0, 2))


def solution(mesh):
    return jax.shard_map(
        functools.partial(per_device, mesh.shape["sink"] // 2, mesh.shape["src"]),
        mesh=mesh,
        in_specs=(
            P(("sink", "src"), None, None),
            P(("sink", "src"), None),
            P("sink", "src", None, None),
            P("sink", "src"),
        ),
        out_specs=P(("sink", "src"), None, None),
        check_vma=False,
    )
```

```python
import functools
import math

import jax
import jax.numpy as jnp
from jax import lax
from jax.experimental import pallas as pl
from jax.experimental.pallas import tpu as pltpu
from jax.sharding import PartitionSpec as P

F32 = jnp.float32
BF16 = jnp.bfloat16
SOFTEN = 0.09
LEAF_DEV = 8
CELLS = 128
PAIR_CAP = 256
FIELDS = 32
FORCES = 24
UNROLL = 4
GRAVITY = 0.05
FALLOFF = 0.16
TWO_ROOT_PI = 1.1283791670955126
FACTOR = GRAVITY * FALLOFF**1.5


def pair_weight(dist_sq):
    square = dist_sq * FALLOFF
    inverse = lax.rsqrt(square)
    tail = 1.0 - lax.erf(square * inverse)
    bell = jnp.exp2(dist_sq * (-FALLOFF / math.log(2.0)))
    return (tail * inverse + bell * TWO_ROOT_PI) * (inverse * inverse)


def place():
    return lax.axis_index("sink"), lax.axis_index("src")


def greet(peers, meanwhile):
    barrier = pltpu.get_barrier_semaphore()
    for peer in peers:
        pl.semaphore_signal(
            barrier, inc=1, device_id=peer, device_id_type=pl.DeviceIdType.MESH
        )
    meanwhile()
    pl.semaphore_wait(barrier, len(peers))


def peers_of(chips, group):
    sink, src = place()
    core = lax.rem(sink, 2)
    half = sink // chips
    steps = sorted(range(1, chips // 2), key=lambda o: -min(o, chips // 2 - o))
    rows = sorted(range(group), key=lambda o: -min(o, group - o))
    return sink, src, core, half, steps, rows


def ringed(sink, chips, step):
    return lax.rem(lax.rem(sink, chips) // 2 + step, chips // 2)


def moved(sink, chips, step):
    return sink // chips * chips + ringed(sink, chips, step) * 2 + lax.rem(sink, 2)


def remote(source, target, send, recv, device):
    return pltpu.make_async_remote_copy(
        src_ref=source,
        dst_ref=target,
        send_sem=send,
        recv_sem=recv,
        device_id=device,
        device_id_type=pl.DeviceIdType.MESH,
    )


def compact(chips, group, core, half, ids, w):
    a = jnp.concatenate([ids[w, 0:1, :], ids[w, 2:3, :]], axis=1)
    b = jnp.concatenate([ids[w, 1:2, :], ids[w, 3:4, :]], axis=1)
    count = jnp.concatenate([ids[w, 4:5, :], ids[w, 5:6, :]], axis=1)
    owner = b // (LEAF_DEV * group)
    slot = lax.broadcasted_iota(jnp.int32, (1, PAIR_CAP), 1)
    chosen = (slot < count) & (owner % 2 == core) & (owner // chips == half)
    flag = jnp.where(chosen, 1.0, 0.0)
    sink = (w * group * LEAF_DEV + a % (group * LEAF_DEV)).astype(F32)
    source = (owner % chips // 2 * LEAF_DEV + b % LEAF_DEV).astype(F32)
    row = lax.broadcasted_iota(jnp.int32, (PAIR_CAP, PAIR_CAP), 0)
    lane = lax.broadcasted_iota(jnp.int32, (PAIR_CAP, PAIR_CAP), 1)
    before = jnp.where(row < lane, 1.0, 0.0).astype(BF16)
    flags = jnp.broadcast_to(flag, (16, PAIR_CAP)).astype(BF16)
    order = jnp.dot(flags, before, preferred_element_type=F32)[0:1, :]
    order = jnp.where(chosen, order, -1.0)
    pick = jnp.where(row.astype(F32) == order, 1.0, 0.0).astype(BF16)
    values = jnp.concatenate(
        [jnp.broadcast_to(sink, (8, PAIR_CAP)), jnp.broadcast_to(source, (8, PAIR_CAP))], axis=0
    ).astype(BF16)
    packed = lax.dot_general(
        values, pick, (((1,), (1,)), ((), ())), preferred_element_type=F32
    ).astype(jnp.int32)
    total = jnp.sum(flag, axis=1, keepdims=True).astype(jnp.int32)
    return packed[0:1, :] * 64 + packed[8:9, :], total


def gather_kernel(
    chips, group, pos, mass, ids, count, column_out, codes, rows_out, choose,
    ids_out, pack, ids_in, load, column_send, column_recv, row_send, row_recv,
    hand_send, hand_recv, own_send, own_recv,
):
    sink, src, core, half, steps, rows = peers_of(chips, group)
    other = 1 - core
    across = lax.rem(sink + chips, 2 * chips)
    partner = (sink + 1 - 2 * core, src)
    diagonal = (across + 1 - 2 * core, src)
    column = [(moved(sink, chips, step), src) for step in steps]
    row = [
        (h, o, (across if h else sink, lax.rem(src + o, group)))
        for o in rows for h in (1, 0) if (h, o) != (0, 0)
    ]
    loads = [
        pltpu.make_async_copy(source, target, load.at[i])
        for i, (source, target) in enumerate((
            (pos, pack.at[0:3]), (mass, pack.at[3]), (ids, ids_in),
        ))
    ]
    for copy in loads:
        copy.start()
    mine = core * 2 + half

    def own_block():
        for copy in loads:
            copy.wait()
        ids_out[mine, 0:2, :] = ids_in[0, 0, :, 0:128]
        ids_out[mine, 2:4, :] = ids_in[0, 0, :, 128:256]
        ids_out[mine, 4:8, :] = jnp.full((4, CELLS), count[0, 0], jnp.int32)
        column_out[ringed(sink, chips, 0)] = pack[...]
        rows_out[mine, src] = pack[...]
        depth = lax.broadcasted_iota(jnp.int32, (96, 512), 0)
        field = lax.broadcasted_iota(jnp.int32, (96, 512), 1) // 128
        for k in range(8):
            hit = (depth % 32 // 8 == field) & (depth % 8 == k)
            choose[k] = jnp.where(hit, 1.0, 0.0).astype(BF16)

    greet(column + [peer for h, o, peer in row] + [partner, diagonal], own_block)

    sends = []

    def start(copy):
        copy.start()
        sends.append(copy)

    for i, peer in enumerate(column):
        start(remote(pack, column_out.at[ringed(sink, chips, 0)], column_send.at[i], column_recv.at[i], peer))
    for i, (h, o, peer) in enumerate(row):
        start(remote(pack, rows_out.at[mine, src], row_send.at[i], row_recv.at[i], peer))
    start(remote(pack, rows_out.at[mine, src], own_send.at[0], own_recv.at[0], partner))
    pool = [partner, (across, src), diagonal]
    for i, peer in enumerate(pool):
        start(remote(ids_out.at[mine], ids_out.at[mine], own_send.at[1 + i], own_recv.at[1 + i], peer))

    for i, (h, o, peer) in reversed(list(enumerate(row))):
        block = rows_out.at[core * 2 + lax.rem(half + h, 2), lax.rem(src + group - o, group)]
        remote(pack, block, row_send.at[i], row_recv.at[i], partner).wait_recv()
        start(remote(block, block, hand_send.at[i], hand_recv.at[i], partner))

    origins = [other * 2 + half, core * 2 + 1 - half, other * 2 + 1 - half]
    for i, origin in enumerate(origins):
        remote(ids_out.at[mine], ids_out.at[origin], own_send.at[1 + i], own_recv.at[1 + i], partner).wait_recv()
    for w in range(4):
        code, total = compact(chips, group, core, half, ids_out, w)
        codes[2 * w : 2 * w + 1, :] = code[:, 0:128]
        codes[2 * w + 1 : 2 * w + 2, :] = code[:, 128:256]
        codes[8 + w : 9 + w, :] = jnp.broadcast_to(total, (1, CELLS))
    codes[12:16, :] = jnp.zeros((4, CELLS), jnp.int32)

    for i, step in reversed(list(enumerate(steps))):
        block = column_out.at[ringed(sink, chips, chips // 2 - step)]
        remote(pack, block, column_send.at[i], column_recv.at[i], partner).wait_recv()
    remote(pack, rows_out.at[other * 2 + half, src], own_send.at[0], own_recv.at[0], partner).wait_recv()
    for i, (h, o, peer) in reversed(list(enumerate(row))):
        block = rows_out.at[other * 2 + lax.rem(half + h, 2), lax.rem(src + group - o, group)]
        remote(pack, block, hand_send.at[i], hand_recv.at[i], partner).wait_recv()
    for copy in sends:
        copy.wait_send()


def thirds(block):
    high = block.astype(BF16).astype(F32)
    rest = block - high
    middle = rest.astype(BF16).astype(F32)
    return high, middle, rest - middle


def pair_kernel(
    group, ring, ids, rows, column, choose, row_force, acc, parts, lines, first_x, second_x
):
    starts = [0]
    for w in range(4):
        starts.append(starts[w] + ids[8 + w, 0])
    every = starts[4]
    last = jnp.maximum(every - 1, 0)
    row_force[...] = jnp.zeros_like(row_force)
    acc[...] = jnp.zeros_like(acc)

    for h in range(ring):
        block = column[h].reshape(FIELDS, CELLS)
        stacked = jnp.concatenate([*thirds(block), jnp.ones_like(block)], axis=0)
        parts[h] = stacked.T.astype(BF16)
    for w in range(4):

        @pl.when(starts[w] < starts[w + 1])
        def _(w=w):
            for h in range(group):
                for i, third in enumerate(thirds(-rows[w, h, 0:3])):
                    lines[i, w * group + h] = third

    sub = lax.broadcasted_iota(jnp.int32, (8, CELLS), 0)
    lane = lax.broadcasted_iota(jnp.int32, (8, CELLS), 1)

    def look(slot):
        slot = jnp.minimum(slot, last)
        shift = 0
        for w in range(1, 4):
            shift = jnp.where(slot >= starts[w], w * PAIR_CAP - starts[w], shift)
        slot = slot + shift
        return ids[slot >> 7, slot & 127]

    def fill(target, first):
        for u in range(UNROLL):
            code = look(first + u)
            sink_block, k = code >> 9, code >> 6 & 7
            tops = []
            for c in range(3):
                high, middle, low = (
                    jnp.broadcast_to(lines[i, sink_block, c, pl.ds(k, 1), :], (8, CELLS))
                    for i in range(3)
                )
                tops.append(
                    jnp.where(
                        sub == 0, high, jnp.where(sub == 1, middle, jnp.where(sub == 2, low, 0.0))
                    )
                )
            top = jnp.concatenate(tops + [jnp.zeros((8, CELLS), F32)], axis=1)
            under = jnp.concatenate([top, jnp.zeros((8, 512), F32)], axis=0).astype(BF16)
            rhs = jnp.concatenate([choose[code & 7], under, jnp.zeros((16, 512), BF16)], axis=0)
            target[u] = jnp.dot(parts[code >> 3 & 7], rhs, preferred_element_type=F32)

    def use(spread, first):
        done = []
        for u in range(UNROLL):
            code = look(first + u)
            sink_block, k = code >> 9, code >> 6 & 7
            live = jnp.where(first + u < every, FACTOR, 0.0)
            at = (code >> 3 & 3) * 32 + (code & 7)
            sink_mass = jnp.broadcast_to(
                rows[sink_block // group, sink_block % group, 3, pl.ds(k, 1), :], (8, CELLS)
            )
            mass = sink_mass * live
            masks = [lane == at + 8 * c for c in range(3)]
            sink_sum = [jnp.zeros((8, CELLS), F32) for _ in range(3)]
            source_sum = []
            for i in range(0, CELLS, 8):
                offset = [spread[u, i : i + 8, 128 * c : 128 * c + 128] for c in range(3)]
                source_mass = spread[u, i : i + 8, 384:512]
                dist_sq = (offset[0] * offset[0] + offset[1] * offset[1]) + (
                    offset[2] * offset[2] + SOFTEN
                )
                weight = (pair_weight(dist_sq) * source_mass) * mass
                force = [weight * offset[c] for c in range(3)]
                sink_sum = [sink_sum[c] + force[c] for c in range(3)]
                total = [jnp.sum(force[c], axis=1, keepdims=True) for c in range(3)]
                source_sum.append(
                    jnp.where(
                        masks[0],
                        total[0],
                        jnp.where(masks[1], total[1], jnp.where(masks[2], total[2], 0.0)),
                    )
                )
            done.append((code >> 5 & 1, sink_block, k, sink_sum, source_sum))
        for g, sink_block, k, sink_sum, source_sum in done:
            for i, value in enumerate(source_sum):
                acc[g, pl.ds(8 * i, 8), :] -= value
            for c in range(3):
                row_force[sink_block, pl.ds(8 * c + k, 1), :] += jnp.sum(
                    sink_sum[c], axis=0, keepdims=True
                )

    fill(first_x, 0)

    def turn(i, carry):
        first = i * (2 * UNROLL)
        fill(second_x, first + UNROLL)
        use(first_x, first)
        fill(first_x, first + 2 * UNROLL)
        use(second_x, first + UNROLL)
        return carry

    lax.fori_loop(0, (every + 2 * UNROLL - 1) // (2 * UNROLL), turn, 0)


def reduce_kernel(
    chips, group, row_force, acc, out,
    column_force, row_sum, row_in, column_in, swap_row,
    column_send, column_recv, row_send, row_recv, swap_send, swap_recv,
):
    sink, src, core, half, steps, rows = peers_of(chips, group)
    other = 1 - core
    across = lax.rem(sink + chips, 2 * chips)
    partner = (sink + 1 - 2 * core, src)
    column = [(moved(sink, chips, step), src) for step in steps]
    row = [
        (h, o, (across if h else sink, lax.rem(src + o, group)))
        for o in rows for h in (1, 0) if (h, o) != (0, 0)
    ]

    def turn_column():
        for g in range(chips // 8):
            turned = acc[g].T
            for h in range(4):
                column_force[g * 4 + h] = turned[32 * h : 32 * h + FORCES, :]

    greet(column + [peer for h, o, peer in row] + [partner], turn_column)
    to_row = remote(
        row_force.at[pl.ds(other * 2 * group, 2 * group)], swap_row, swap_send.at[0], swap_recv.at[0], partner
    )
    to_row.start()
    sends = [to_row]
    for i, peer in enumerate(column):
        copy = remote(
            column_force.at[ringed(sink, chips, steps[i])], column_in.at[i], column_send.at[i], column_recv.at[i], peer
        )
        copy.start()
        sends.append(copy)
    to_row.wait_recv()
    row_sum[...] = row_force[pl.ds(core * 2 * group, 2 * group)] + swap_row[...]
    for i, (h, o, peer) in enumerate(row):
        copy = remote(
            row_sum.at[lax.rem(half + h, 2) * group + peer[1]], row_in.at[i],
            row_send.at[i], row_recv.at[i], peer,
        )
        copy.start()
        sends.append(copy)
    total = column_force[ringed(sink, chips, 0)] + row_sum[half * group + src]
    for i in reversed(range(len(row))):
        remote(row_sum.at[0], row_in.at[i], row_send.at[i], row_recv.at[i], partner).wait_recv()
        total = total + row_in[i]
    for i in reversed(range(len(column))):
        remote(column_force.at[0], column_in.at[i], column_send.at[i], column_recv.at[i], partner).wait_recv()
        total = total + column_in[i]
    out[...] = total.reshape(3, LEAF_DEV, CELLS)
    for copy in sends:
        copy.wait_send()


def per_device(chips, group, leaf_pos, leaf_mass, pair_ids, pair_count):
    vmem = pl.BlockSpec(memory_space=pltpu.VMEM)
    smem = pl.BlockSpec(memory_space=pltpu.SMEM)
    hbm = pl.BlockSpec(memory_space=pltpu.HBM)
    dma = pltpu.SemaphoreType.DMA
    ring = chips // 2
    column, codes, rows, choose = pl.pallas_call(
        functools.partial(gather_kernel, chips, group),
        name="gather",
        out_shape=(
            jax.ShapeDtypeStruct((ring, 4, LEAF_DEV, CELLS), F32),
            jax.ShapeDtypeStruct((16, CELLS), jnp.int32),
            jax.ShapeDtypeStruct((4, group, 4, LEAF_DEV, CELLS), F32),
            jax.ShapeDtypeStruct((8, 96, 512), BF16),
        ),
        in_specs=[hbm] * 3 + [smem],
        out_specs=(vmem,) * 4,
        scratch_shapes=[
            pltpu.VMEM((4, 8, CELLS), jnp.int32),
            pltpu.VMEM((4, LEAF_DEV, CELLS), F32),
            pltpu.VMEM((1, 1, 2, PAIR_CAP), jnp.int32),
            dma((3,)),
            dma((ring - 1,)), dma((ring - 1,)),
            dma((2 * group - 1,)), dma((2 * group - 1,)),
            dma((2 * group - 1,)), dma((2 * group - 1,)),
            dma((4,)), dma((4,)),
        ],
        compiler_params=pltpu.CompilerParams(
            collective_id=0, has_side_effects=True, vmem_limit_bytes=16 << 20
        ),
    )(*(
        pltpu.with_memory_space_constraint(x, pltpu.HBM)
        for x in (jnp.transpose(leaf_pos, (1, 0, 2)), leaf_mass, pair_ids)
    ), pair_count)
    row_force, acc = pl.pallas_call(
        functools.partial(pair_kernel, group, ring),
        name="pairs",
        out_shape=(
            jax.ShapeDtypeStruct((4 * group, FORCES, CELLS), F32),
            jax.ShapeDtypeStruct((ring // 4, 128, CELLS), F32),
        ),
        in_specs=[smem, vmem, vmem, vmem],
        out_specs=(vmem, vmem),
        scratch_shapes=[
            pltpu.VMEM((ring, 128, 128), BF16),
            pltpu.VMEM((3, 4 * group, 3, LEAF_DEV, CELLS), F32),
            pltpu.VMEM((UNROLL, 128, 512), F32),
            pltpu.VMEM((UNROLL, 128, 512), F32),
        ],
        compiler_params=pltpu.CompilerParams(vmem_limit_bytes=40 << 20),
    )(codes, rows, column, choose)
    force = pl.pallas_call(
        functools.partial(reduce_kernel, chips, group),
        name="reduce",
        out_shape=jax.ShapeDtypeStruct((3, LEAF_DEV, CELLS), F32),
        in_specs=[vmem, vmem],
        out_specs=vmem,
        scratch_shapes=[
            pltpu.VMEM((ring, FORCES, CELLS), F32),
            pltpu.VMEM((2 * group, FORCES, CELLS), F32),
            pltpu.VMEM((2 * group - 1, FORCES, CELLS), F32),
            pltpu.VMEM((ring - 1, FORCES, CELLS), F32),
            pltpu.VMEM((2 * group, FORCES, CELLS), F32),
            dma((ring - 1,)), dma((ring - 1,)),
            dma((2 * group - 1,)), dma((2 * group - 1,)),
            dma((1,)), dma((1,)),
        ],
        compiler_params=pltpu.CompilerParams(
            collective_id=1, has_side_effects=True, vmem_limit_bytes=16 << 20
        ),
    )(row_force, acc)
    return jnp.transpose(force, (1, 0, 2))


def solution(mesh):
    return jax.shard_map(
        functools.partial(per_device, mesh.shape["sink"] // 2, mesh.shape["src"]),
        mesh=mesh,
        in_specs=(
            P(("sink", "src"), None, None),
            P(("sink", "src"), None),
            P("sink", "src", None, None),
            P("sink", "src"),
        ),
        out_specs=P(("sink", "src"), None, None),
        check_vma=False,
    )
```

```python
import functools
import math

import jax
import jax.numpy as jnp
from jax import lax
from jax.experimental import pallas as pl
from jax.experimental.pallas import tpu as pltpu
from jax.sharding import PartitionSpec as P

F32 = jnp.float32
BF16 = jnp.bfloat16
SOFTEN = 0.09
LEAF_DEV = 8
CELLS = 128
PAIR_CAP = 256
FIELDS = 32
FORCES = 24
UNROLL = 4
GRAVITY = 0.05
FALLOFF = 0.16
TWO_ROOT_PI = 1.1283791670955126
FACTOR = GRAVITY * FALLOFF**1.5


def pair_weight(dist_sq):
    square = dist_sq * FALLOFF
    inverse = lax.rsqrt(square)
    tail = 1.0 - lax.erf(square * inverse)
    bell = jnp.exp2(dist_sq * (-FALLOFF / math.log(2.0)))
    return (tail * inverse + bell * TWO_ROOT_PI) * (inverse * inverse)


def place():
    return lax.axis_index("sink"), lax.axis_index("src")


def greet(peers, meanwhile):
    barrier = pltpu.get_barrier_semaphore()
    for peer in peers:
        pl.semaphore_signal(
            barrier, inc=1, device_id=peer, device_id_type=pl.DeviceIdType.MESH
        )
    meanwhile()
    pl.semaphore_wait(barrier, len(peers))


def peers_of(chips, group):
    sink, src = place()
    core = lax.rem(sink, 2)
    half = sink // chips
    steps = sorted(range(1, chips // 2), key=lambda o: -min(o, chips // 2 - o))
    rows = sorted(range(group), key=lambda o: -min(o, group - o))
    return sink, src, core, half, steps, rows


def ringed(sink, chips, step):
    return lax.rem(lax.rem(sink, chips) // 2 + step, chips // 2)


def moved(sink, chips, step):
    return sink // chips * chips + ringed(sink, chips, step) * 2 + lax.rem(sink, 2)


def remote(source, target, send, recv, device):
    return pltpu.make_async_remote_copy(
        src_ref=source,
        dst_ref=target,
        send_sem=send,
        recv_sem=recv,
        device_id=device,
        device_id_type=pl.DeviceIdType.MESH,
    )


def compact(chips, group, core, half, ids, w):
    a = jnp.concatenate([ids[w, 0:1, :], ids[w, 2:3, :]], axis=1)
    b = jnp.concatenate([ids[w, 1:2, :], ids[w, 3:4, :]], axis=1)
    count = jnp.concatenate([ids[w, 4:5, :], ids[w, 5:6, :]], axis=1)
    owner = b // (LEAF_DEV * group)
    slot = lax.broadcasted_iota(jnp.int32, (1, PAIR_CAP), 1)
    chosen = (slot < count) & (owner % 2 == core) & (owner // chips == half)
    flag = jnp.where(chosen, 1.0, 0.0)
    sink = (w * group * LEAF_DEV + a % (group * LEAF_DEV)).astype(F32)
    source = (owner % chips // 2 * LEAF_DEV + b % LEAF_DEV).astype(F32)
    row = lax.broadcasted_iota(jnp.int32, (PAIR_CAP, PAIR_CAP), 0)
    lane = lax.broadcasted_iota(jnp.int32, (PAIR_CAP, PAIR_CAP), 1)
    before = jnp.where(row < lane, 1.0, 0.0).astype(BF16)
    flags = jnp.broadcast_to(flag, (16, PAIR_CAP)).astype(BF16)
    order = jnp.dot(flags, before, preferred_element_type=F32)[0:1, :]
    order = jnp.where(chosen, order, -1.0)
    pick = jnp.where(row.astype(F32) == order, 1.0, 0.0).astype(BF16)
    values = jnp.concatenate(
        [jnp.broadcast_to(sink, (8, PAIR_CAP)), jnp.broadcast_to(source, (8, PAIR_CAP))], axis=0
    ).astype(BF16)
    packed = lax.dot_general(
        values, pick, (((1,), (1,)), ((), ())), preferred_element_type=F32
    ).astype(jnp.int32)
    total = jnp.sum(flag, axis=1, keepdims=True).astype(jnp.int32)
    return packed[0:1, :] * 64 + packed[8:9, :], total


def gather_kernel(
    chips, group, pos, mass, ids, count, column_out, codes, rows_out, choose,
    ids_out, pack, ids_in, load, column_send, column_recv, row_send, row_recv,
    hand_send, hand_recv, own_send, own_recv,
):
    sink, src, core, half, steps, rows = peers_of(chips, group)
    other = 1 - core
    across = lax.rem(sink + chips, 2 * chips)
    partner = (sink + 1 - 2 * core, src)
    diagonal = (across + 1 - 2 * core, src)
    column = [(moved(sink, chips, step), src) for step in steps]
    row = [
        (h, o, (across if h else sink, lax.rem(src + o, group)))
        for o in rows for h in (1, 0) if (h, o) != (0, 0)
    ]
    loads = [
        pltpu.make_async_copy(source, target, load.at[i])
        for i, (source, target) in enumerate((
            (pos, pack.at[0:3]), (mass, pack.at[3]), (ids, ids_in),
        ))
    ]
    for copy in loads:
        copy.start()
    mine = core * 2 + half

    def own_block():
        for copy in loads:
            copy.wait()
        ids_out[mine, 0:2, :] = ids_in[0, 0, :, 0:128]
        ids_out[mine, 2:4, :] = ids_in[0, 0, :, 128:256]
        ids_out[mine, 4:8, :] = jnp.full((4, CELLS), count[0, 0], jnp.int32)
        column_out[ringed(sink, chips, 0)] = pack[...]
        rows_out[mine, src] = pack[...]
        depth = lax.broadcasted_iota(jnp.int32, (96, 512), 0)
        field = lax.broadcasted_iota(jnp.int32, (96, 512), 1) // 128
        for k in range(8):
            hit = (depth % 32 // 8 == field) & (depth % 8 == k)
            choose[k] = jnp.where(hit, 1.0, 0.0).astype(BF16)

    greet([peer for h, o, peer in row] + column + [diagonal, partner], own_block)

    sends = []

    def start(copy):
        copy.start()
        sends.append(copy)

    for i, (h, o, peer) in enumerate(row):
        start(remote(pack, rows_out.at[mine, src], row_send.at[i], row_recv.at[i], peer))
    start(remote(pack, rows_out.at[mine, src], own_send.at[0], own_recv.at[0], partner))
    pool = [partner, (across, src), diagonal]
    for i, peer in enumerate(pool):
        start(remote(ids_out.at[mine], ids_out.at[mine], own_send.at[1 + i], own_recv.at[1 + i], peer))
    for i, peer in enumerate(column):
        start(remote(pack, column_out.at[ringed(sink, chips, 0)], column_send.at[i], column_recv.at[i], peer))

    for i, (h, o, peer) in enumerate(row):
        block = rows_out.at[core * 2 + lax.rem(half + h, 2), lax.rem(src + group - o, group)]
        remote(pack, block, row_send.at[i], row_recv.at[i], partner).wait_recv()
        start(remote(block, block, hand_send.at[i], hand_recv.at[i], partner))

    origins = [other * 2 + half, core * 2 + 1 - half, other * 2 + 1 - half]
    for i, origin in enumerate(origins):
        remote(ids_out.at[mine], ids_out.at[origin], own_send.at[1 + i], own_recv.at[1 + i], partner).wait_recv()
    for w in range(4):
        code, total = compact(chips, group, core, half, ids_out, w)
        codes[2 * w : 2 * w + 1, :] = code[:, 0:128]
        codes[2 * w + 1 : 2 * w + 2, :] = code[:, 128:256]
        codes[8 + w : 9 + w, :] = jnp.broadcast_to(total, (1, CELLS))
    codes[12:16, :] = jnp.zeros((4, CELLS), jnp.int32)

    for i, step in reversed(list(enumerate(steps))):
        block = column_out.at[ringed(sink, chips, chips // 2 - step)]
        remote(pack, block, column_send.at[i], column_recv.at[i], partner).wait_recv()
    remote(pack, rows_out.at[other * 2 + half, src], own_send.at[0], own_recv.at[0], partner).wait_recv()
    for i, (h, o, peer) in reversed(list(enumerate(row))):
        block = rows_out.at[other * 2 + lax.rem(half + h, 2), lax.rem(src + group - o, group)]
        remote(pack, block, hand_send.at[i], hand_recv.at[i], partner).wait_recv()
    for copy in sends:
        copy.wait_send()


def thirds(block):
    high = block.astype(BF16).astype(F32)
    rest = block - high
    middle = rest.astype(BF16).astype(F32)
    return high, middle, rest - middle


def pair_kernel(
    group, ring, ids, rows, column, choose, row_force, acc, parts, lines, first_x, second_x
):
    starts = [0]
    for w in range(4):
        starts.append(starts[w] + ids[8 + w, 0])
    every = starts[4]
    last = jnp.maximum(every - 1, 0)
    row_force[...] = jnp.zeros_like(row_force)
    acc[...] = jnp.zeros_like(acc)

    for h in range(ring):
        block = column[h].reshape(FIELDS, CELLS)
        stacked = jnp.concatenate([*thirds(block), jnp.ones_like(block)], axis=0)
        parts[h] = stacked.T.astype(BF16)
    for w in range(4):

        @pl.when(starts[w] < starts[w + 1])
        def _(w=w):
            for h in range(group):
                for i, third in enumerate(thirds(-rows[w, h, 0:3])):
                    lines[i, w * group + h] = third

    sub = lax.broadcasted_iota(jnp.int32, (8, CELLS), 0)
    lane = lax.broadcasted_iota(jnp.int32, (8, CELLS), 1)

    def look(slot):
        slot = jnp.minimum(slot, last)
        shift = 0
        for w in range(1, 4):
            shift = jnp.where(slot >= starts[w], w * PAIR_CAP - starts[w], shift)
        slot = slot + shift
        return ids[slot >> 7, slot & 127]

    def fill(target, first):
        for u in range(UNROLL):
            code = look(first + u)
            sink_block, k = code >> 9, code >> 6 & 7
            tops = []
            for c in range(3):
                high, middle, low = (
                    jnp.broadcast_to(lines[i, sink_block, c, pl.ds(k, 1), :], (8, CELLS))
                    for i in range(3)
                )
                tops.append(
                    jnp.where(
                        sub == 0, high, jnp.where(sub == 1, middle, jnp.where(sub == 2, low, 0.0))
                    )
                )
            top = jnp.concatenate(tops + [jnp.zeros((8, CELLS), F32)], axis=1)
            under = jnp.concatenate([top, jnp.zeros((8, 512), F32)], axis=0).astype(BF16)
            rhs = jnp.concatenate([choose[code & 7], under, jnp.zeros((16, 512), BF16)], axis=0)
            for n in (0, 256):
                target[u, :, n : n + 256] = jnp.dot(parts[code >> 3 & 7], rhs[:, n : n + 256], preferred_element_type=F32)

    def use(spread, first):
        done = []
        for u in range(UNROLL):
            code = look(first + u)
            sink_block, k = code >> 9, code >> 6 & 7
            live = jnp.where(first + u < every, FACTOR, 0.0)
            at = (code >> 3 & 3) * 32 + (code & 7)
            sink_mass = jnp.broadcast_to(
                rows[sink_block // group, sink_block % group, 3, pl.ds(k, 1), :], (8, CELLS)
            )
            mass = sink_mass * live
            masks = [lane == at + 8 * c for c in range(3)]
            sink_sum = [jnp.zeros((8, CELLS), F32) for _ in range(3)]
            source_sum = []
            for i in range(0, CELLS, 8):
                offset = [spread[u, i : i + 8, 128 * c : 128 * c + 128] for c in range(3)]
                source_mass = spread[u, i : i + 8, 384:512]
                dist_sq = (offset[0] * offset[0] + offset[1] * offset[1]) + (
                    offset[2] * offset[2] + SOFTEN
                )
                weight = (pair_weight(dist_sq) * source_mass) * mass
                force = [weight * offset[c] for c in range(3)]
                sink_sum = [sink_sum[c] + force[c] for c in range(3)]
                total = [jnp.sum(force[c], axis=1, keepdims=True) for c in range(3)]
                source_sum.append(
                    jnp.where(
                        masks[0],
                        total[0],
                        jnp.where(masks[1], total[1], jnp.where(masks[2], total[2], 0.0)),
                    )
                )
            done.append((code >> 5 & 1, sink_block, k, sink_sum, source_sum))
        for g, sink_block, k, sink_sum, source_sum in done:
            for i, value in enumerate(source_sum):
                acc[g, pl.ds(8 * i, 8), :] -= value
            for c in range(3):
                row_force[sink_block, pl.ds(8 * c + k, 1), :] += jnp.sum(
                    sink_sum[c], axis=0, keepdims=True
                )

    fill(first_x, 0)
    fill(second_x, UNROLL)

    def turn(i, carry):
        first = i * (2 * UNROLL)
        use(first_x, first)
        fill(first_x, first + 2 * UNROLL)
        use(second_x, first + UNROLL)
        fill(second_x, first + 3 * UNROLL)
        return carry

    turns = every // (2 * UNROLL)
    lax.fori_loop(0, turns, turn, 0)
    done = turns * (2 * UNROLL)

    @pl.when(done < every)
    def _():
        use(first_x, done)

    @pl.when(done + UNROLL < every)
    def _():
        use(second_x, done + UNROLL)


def reduce_kernel(
    chips, group, row_force, acc, out,
    column_force, row_sum, row_in, column_in, swap_row,
    column_send, column_recv, row_send, row_recv, swap_send, swap_recv,
):
    sink, src, core, half, steps, rows = peers_of(chips, group)
    other = 1 - core
    across = lax.rem(sink + chips, 2 * chips)
    partner = (sink + 1 - 2 * core, src)
    column = [(moved(sink, chips, step), src) for step in steps]
    row = [
        (h, o, (across if h else sink, lax.rem(src + o, group)))
        for o in rows for h in (1, 0) if (h, o) != (0, 0)
    ]

    def turn_column():
        for g in range(chips // 8):
            turned = acc[g].T
            for h in range(4):
                column_force[g * 4 + h] = turned[32 * h : 32 * h + FORCES, :]

    greet([peer for h, o, peer in row] + column + [partner], turn_column)
    order = [(h, o) for h, o, peer in row] + [(0, 0)]
    blocks = [(lax.rem(half + h, 2) * group, lax.rem(src + o, group)) for h, o in order]
    swaps = [
        remote(
            row_force.at[other * 2 * group + line + at], swap_row.at[i],
            swap_send.at[i], swap_recv.at[i], partner,
        )
        for i, (line, at) in enumerate(blocks)
    ]
    sends = list(swaps)
    for copy in swaps:
        copy.start()
    for i, peer in enumerate(column):
        copy = remote(
            column_force.at[ringed(sink, chips, steps[i])], column_in.at[i],
            column_send.at[i], column_recv.at[i], peer,
        )
        copy.start()
        sends.append(copy)
    for i, (line, at) in enumerate(blocks):
        swaps[i].wait_recv()
        row_sum[i] = row_force[core * 2 * group + line + at] + swap_row[i]
        if i < len(row):
            copy = remote(row_sum.at[i], row_in.at[i], row_send.at[i], row_recv.at[i], row[i][2])
            copy.start()
            sends.append(copy)
    total = column_force[ringed(sink, chips, 0)] + row_sum[len(row)]
    for i in reversed(range(len(row))):
        remote(row_sum.at[0], row_in.at[i], row_send.at[i], row_recv.at[i], partner).wait_recv()
        total = total + row_in[i]
    for i in reversed(range(len(column))):
        remote(column_force.at[0], column_in.at[i], column_send.at[i], column_recv.at[i], partner).wait_recv()
        total = total + column_in[i]
    out[...] = total.reshape(3, LEAF_DEV, CELLS)
    for copy in sends:
        copy.wait_send()


def per_device(chips, group, leaf_pos, leaf_mass, pair_ids, pair_count):
    vmem = pl.BlockSpec(memory_space=pltpu.VMEM)
    smem = pl.BlockSpec(memory_space=pltpu.SMEM)
    hbm = pl.BlockSpec(memory_space=pltpu.HBM)
    dma = pltpu.SemaphoreType.DMA
    ring = chips // 2
    column, codes, rows, choose = pl.pallas_call(
        functools.partial(gather_kernel, chips, group),
        name="gather",
        out_shape=(
            jax.ShapeDtypeStruct((ring, 4, LEAF_DEV, CELLS), F32),
            jax.ShapeDtypeStruct((16, CELLS), jnp.int32),
            jax.ShapeDtypeStruct((4, group, 4, LEAF_DEV, CELLS), F32),
            jax.ShapeDtypeStruct((8, 96, 512), BF16),
        ),
        in_specs=[hbm] * 3 + [smem],
        out_specs=(vmem,) * 4,
        scratch_shapes=[
            pltpu.VMEM((4, 8, CELLS), jnp.int32),
            pltpu.VMEM((4, LEAF_DEV, CELLS), F32),
            pltpu.VMEM((1, 1, 2, PAIR_CAP), jnp.int32),
            dma((3,)),
            dma((ring - 1,)), dma((ring - 1,)),
            dma((2 * group - 1,)), dma((2 * group - 1,)),
            dma((2 * group - 1,)), dma((2 * group - 1,)),
            dma((4,)), dma((4,)),
        ],
        compiler_params=pltpu.CompilerParams(
            collective_id=0, has_side_effects=True, vmem_limit_bytes=16 << 20
        ),
    )(*(
        pltpu.with_memory_space_constraint(x, pltpu.HBM)
        for x in (jnp.transpose(leaf_pos, (1, 0, 2)), leaf_mass, pair_ids)
    ), pair_count)
    row_force, acc = pl.pallas_call(
        functools.partial(pair_kernel, group, ring),
        name="pairs",
        out_shape=(
            jax.ShapeDtypeStruct((4 * group, FORCES, CELLS), F32),
            jax.ShapeDtypeStruct((ring // 4, 128, CELLS), F32),
        ),
        in_specs=[smem, vmem, vmem, vmem],
        out_specs=(vmem, vmem),
        scratch_shapes=[
            pltpu.VMEM((ring, 128, 128), BF16),
            pltpu.VMEM((3, 4 * group, 3, LEAF_DEV, CELLS), F32),
            pltpu.VMEM((UNROLL, 128, 512), F32),
            pltpu.VMEM((UNROLL, 128, 512), F32),
        ],
        compiler_params=pltpu.CompilerParams(vmem_limit_bytes=40 << 20),
    )(codes, rows, column, choose)
    force = pl.pallas_call(
        functools.partial(reduce_kernel, chips, group),
        name="reduce",
        out_shape=jax.ShapeDtypeStruct((3, LEAF_DEV, CELLS), F32),
        in_specs=[vmem, vmem],
        out_specs=vmem,
        scratch_shapes=[
            pltpu.VMEM((ring, FORCES, CELLS), F32),
            pltpu.VMEM((2 * group, FORCES, CELLS), F32),
            pltpu.VMEM((2 * group - 1, FORCES, CELLS), F32),
            pltpu.VMEM((ring - 1, FORCES, CELLS), F32),
            pltpu.VMEM((2 * group, FORCES, CELLS), F32),
            dma((ring - 1,)), dma((ring - 1,)),
            dma((2 * group - 1,)), dma((2 * group - 1,)),
            dma((2 * group,)), dma((2 * group,)),
        ],
        compiler_params=pltpu.CompilerParams(
            collective_id=1, has_side_effects=True, vmem_limit_bytes=16 << 20
        ),
    )(row_force, acc)
    return jnp.transpose(force, (1, 0, 2))


def solution(mesh):
    return jax.shard_map(
        functools.partial(per_device, mesh.shape["sink"] // 2, mesh.shape["src"]),
        mesh=mesh,
        in_specs=(
            P(("sink", "src"), None, None),
            P(("sink", "src"), None),
            P("sink", "src", None, None),
            P("sink", "src"),
        ),
        out_specs=P(("sink", "src"), None, None),
        check_vma=False,
    )
```

```python
import functools
import math

import jax
import jax.numpy as jnp
from jax import lax
from jax.experimental import pallas as pl
from jax.experimental.pallas import tpu as pltpu
from jax.sharding import PartitionSpec as P

F32 = jnp.float32
BF16 = jnp.bfloat16
SOFTEN = 0.09
LEAF_DEV = 8
CELLS = 128
PAIR_CAP = 256
FIELDS = 32
FORCES = 24
UNROLL = 4
GRAVITY = 0.05
FALLOFF = 0.16
TWO_ROOT_PI = 1.1283791670955126
FACTOR = GRAVITY * FALLOFF**1.5


def pair_weight(dist_sq):
    square = dist_sq * FALLOFF
    inverse = lax.rsqrt(square)
    tail = 1.0 - lax.erf(square * inverse)
    bell = jnp.exp2(dist_sq * (-FALLOFF / math.log(2.0)) + math.log2(TWO_ROOT_PI))
    return (tail * inverse + bell) * (inverse * inverse)


def place():
    return lax.axis_index("sink"), lax.axis_index("src")


def greet(peers, meanwhile):
    barrier = pltpu.get_barrier_semaphore()
    for peer in peers:
        pl.semaphore_signal(
            barrier, inc=1, device_id=peer, device_id_type=pl.DeviceIdType.MESH
        )
    meanwhile()
    pl.semaphore_wait(barrier, len(peers))


def peers_of(chips, group):
    sink, src = place()
    core = lax.rem(sink, 2)
    half = sink // chips
    steps = sorted(range(1, chips // 2), key=lambda o: -min(o, chips // 2 - o))
    rows = sorted(range(group), key=lambda o: -min(o, group - o))
    return sink, src, core, half, steps, rows


def ringed(sink, chips, step):
    return lax.rem(lax.rem(sink, chips) // 2 + step, chips // 2)


def moved(sink, chips, step):
    return sink // chips * chips + ringed(sink, chips, step) * 2 + lax.rem(sink, 2)


def remote(source, target, send, recv, device):
    return pltpu.make_async_remote_copy(
        src_ref=source,
        dst_ref=target,
        send_sem=send,
        recv_sem=recv,
        device_id=device,
        device_id_type=pl.DeviceIdType.MESH,
    )


def compact(chips, group, core, half, ids, w):
    a = jnp.concatenate([ids[w, 0:1, :], ids[w, 2:3, :]], axis=1)
    b = jnp.concatenate([ids[w, 1:2, :], ids[w, 3:4, :]], axis=1)
    count = jnp.concatenate([ids[w, 4:5, :], ids[w, 5:6, :]], axis=1)
    owner = b // (LEAF_DEV * group)
    slot = lax.broadcasted_iota(jnp.int32, (1, PAIR_CAP), 1)
    chosen = (slot < count) & (owner % 2 == core) & (owner // chips == half)
    flag = jnp.where(chosen, 1.0, 0.0)
    sink = (w * group * LEAF_DEV + a % (group * LEAF_DEV)).astype(F32)
    source = (owner % chips // 2 * LEAF_DEV + b % LEAF_DEV).astype(F32)
    row = lax.broadcasted_iota(jnp.int32, (PAIR_CAP, PAIR_CAP), 0)
    lane = lax.broadcasted_iota(jnp.int32, (PAIR_CAP, PAIR_CAP), 1)
    before = jnp.where(row < lane, 1.0, 0.0).astype(BF16)
    flags = jnp.broadcast_to(flag, (16, PAIR_CAP)).astype(BF16)
    order = jnp.dot(flags, before, preferred_element_type=F32)[0:1, :]
    order = jnp.where(chosen, order, -1.0)
    pick = jnp.where(row.astype(F32) == order, 1.0, 0.0).astype(BF16)
    values = jnp.concatenate(
        [jnp.broadcast_to(sink, (8, PAIR_CAP)), jnp.broadcast_to(source, (8, PAIR_CAP))], axis=0
    ).astype(BF16)
    packed = lax.dot_general(
        values, pick, (((1,), (1,)), ((), ())), preferred_element_type=F32
    ).astype(jnp.int32)
    total = jnp.sum(flag, axis=1, keepdims=True).astype(jnp.int32)
    return packed[0:1, :] * 64 + packed[8:9, :], total


def gather_kernel(
    chips, group, pos, mass, ids, count, column_out, codes, rows_out, choose,
    ids_out, pack, ids_in, load, column_send, column_recv, row_send, row_recv,
    hand_send, hand_recv, own_send, own_recv,
):
    sink, src, core, half, steps, rows = peers_of(chips, group)
    other = 1 - core
    across = lax.rem(sink + chips, 2 * chips)
    partner = (sink + 1 - 2 * core, src)
    diagonal = (across + 1 - 2 * core, src)
    column = [(moved(sink, chips, step), src) for step in steps]
    row = [
        (h, o, (across if h else sink, lax.rem(src + o, group)))
        for o in rows for h in (1, 0) if (h, o) != (0, 0)
    ]
    loads = [
        pltpu.make_async_copy(source, target, load.at[i])
        for i, (source, target) in enumerate((
            (pos, pack.at[0:3]), (mass, pack.at[3]), (ids, ids_in),
        ))
    ]
    for copy in loads:
        copy.start()
    mine = core * 2 + half

    def own_block():
        for copy in loads:
            copy.wait()
        ids_out[mine, 0:2, :] = ids_in[0, 0, :, 0:128]
        ids_out[mine, 2:4, :] = ids_in[0, 0, :, 128:256]
        ids_out[mine, 4:8, :] = jnp.full((4, CELLS), count[0, 0], jnp.int32)
        column_out[ringed(sink, chips, 0)] = pack[...]
        rows_out[mine, src] = pack[...]
        depth = lax.broadcasted_iota(jnp.int32, (96, 512), 0)
        field = lax.broadcasted_iota(jnp.int32, (96, 512), 1) // 128
        for k in range(8):
            hit = (depth % 32 // 8 == field) & (depth % 8 == k)
            choose[k] = jnp.where(hit, 1.0, 0.0).astype(BF16)

    greet([peer for h, o, peer in row] + column + [diagonal, partner], own_block)

    sends = []

    def start(copy):
        copy.start()
        sends.append(copy)

    for i, (h, o, peer) in enumerate(row):
        start(remote(pack, rows_out.at[mine, src], row_send.at[i], row_recv.at[i], peer))
    start(remote(pack, rows_out.at[mine, src], own_send.at[0], own_recv.at[0], partner))
    pool = [partner, (across, src), diagonal]
    for i, peer in enumerate(pool):
        start(remote(ids_out.at[mine], ids_out.at[mine], own_send.at[1 + i], own_recv.at[1 + i], peer))
    for i, peer in enumerate(column):
        start(remote(pack, column_out.at[ringed(sink, chips, 0)], column_send.at[i], column_recv.at[i], peer))

    for i, (h, o, peer) in enumerate(row):
        block = rows_out.at[core * 2 + lax.rem(half + h, 2), lax.rem(src + group - o, group)]
        remote(pack, block, row_send.at[i], row_recv.at[i], partner).wait_recv()
        start(remote(block, block, hand_send.at[i], hand_recv.at[i], partner))

    origins = [other * 2 + half, core * 2 + 1 - half, other * 2 + 1 - half]
    for i, origin in enumerate(origins):
        remote(ids_out.at[mine], ids_out.at[origin], own_send.at[1 + i], own_recv.at[1 + i], partner).wait_recv()
    for w in range(4):
        code, total = compact(chips, group, core, half, ids_out, w)
        codes[2 * w : 2 * w + 1, :] = code[:, 0:128]
        codes[2 * w + 1 : 2 * w + 2, :] = code[:, 128:256]
        codes[8 + w : 9 + w, :] = jnp.broadcast_to(total, (1, CELLS))
    codes[12:16, :] = jnp.zeros((4, CELLS), jnp.int32)

    for i, step in reversed(list(enumerate(steps))):
        block = column_out.at[ringed(sink, chips, chips // 2 - step)]
        remote(pack, block, column_send.at[i], column_recv.at[i], partner).wait_recv()
    remote(pack, rows_out.at[other * 2 + half, src], own_send.at[0], own_recv.at[0], partner).wait_recv()
    for i, (h, o, peer) in reversed(list(enumerate(row))):
        block = rows_out.at[other * 2 + lax.rem(half + h, 2), lax.rem(src + group - o, group)]
        remote(pack, block, hand_send.at[i], hand_recv.at[i], partner).wait_recv()
    for copy in sends:
        copy.wait_send()


def thirds(block):
    high = block.astype(BF16).astype(F32)
    rest = block - high
    middle = rest.astype(BF16).astype(F32)
    return high, middle, rest - middle


def pair_kernel(
    group, ring, ids, rows, column, choose, row_force, acc, parts, lines, first_x, second_x
):
    starts = [0]
    for w in range(4):
        starts.append(starts[w] + ids[8 + w, 0])
    every = starts[4]
    last = jnp.maximum(every - 1, 0)
    row_force[...] = jnp.zeros_like(row_force)
    acc[...] = jnp.zeros_like(acc)

    for h in range(ring):
        block = column[h].reshape(FIELDS, CELLS)
        stacked = jnp.concatenate([*thirds(block), jnp.ones_like(block)], axis=0)
        parts[h] = stacked.T.astype(BF16)
    for w in range(4):

        @pl.when(starts[w] < starts[w + 1])
        def _(w=w):
            for h in range(group):
                for i, third in enumerate(thirds(-rows[w, h, 0:3])):
                    lines[i, w * group + h] = third

    sub = lax.broadcasted_iota(jnp.int32, (8, CELLS), 0)
    lane = lax.broadcasted_iota(jnp.int32, (8, CELLS), 1)

    def look(slot):
        slot = jnp.minimum(slot, last)
        shift = 0
        for w in range(1, 4):
            shift = jnp.where(slot >= starts[w], w * PAIR_CAP - starts[w], shift)
        slot = slot + shift
        return ids[slot >> 7, slot & 127]

    def fill(target, first):
        for u in range(UNROLL):
            code = look(first + u)
            sink_block, k = code >> 9, code >> 6 & 7
            tops = []
            for c in range(3):
                high, middle, low = (
                    jnp.broadcast_to(lines[i, sink_block, c, pl.ds(k, 1), :], (8, CELLS))
                    for i in range(3)
                )
                tops.append(
                    jnp.where(
                        sub == 0, high, jnp.where(sub == 1, middle, jnp.where(sub == 2, low, 0.0))
                    )
                )
            top = jnp.concatenate(tops + [jnp.zeros((8, CELLS), F32)], axis=1)
            under = jnp.concatenate([top, jnp.zeros((8, 512), F32)], axis=0).astype(BF16)
            rhs = jnp.concatenate([choose[code & 7], under, jnp.zeros((16, 512), BF16)], axis=0)
            for n in (0, 256):
                target[u, :, n : n + 256] = jnp.dot(parts[code >> 3 & 7], rhs[:, n : n + 256], preferred_element_type=F32)

    def use(spread, first):
        done = []
        for u in range(UNROLL):
            code = look(first + u)
            sink_block, k = code >> 9, code >> 6 & 7
            live = jnp.where(first + u < every, FACTOR, 0.0)
            at = (code >> 3 & 3) * 32 + (code & 7)
            sink_mass = jnp.broadcast_to(
                rows[sink_block // group, sink_block % group, 3, pl.ds(k, 1), :], (8, CELLS)
            )
            mass = sink_mass * live
            masks = [lane == at + 8 * c for c in range(3)]
            sink_sum = [jnp.zeros((8, CELLS), F32) for _ in range(3)]
            source_sum = []
            for i in range(0, CELLS, 8):
                offset = [spread[u, i : i + 8, 128 * c : 128 * c + 128] for c in range(3)]
                source_mass = spread[u, i : i + 8, 384:512]
                dist_sq = (offset[0] * offset[0] + offset[1] * offset[1]) + (
                    offset[2] * offset[2] + SOFTEN
                )
                weight = (pair_weight(dist_sq) * source_mass) * mass
                force = [weight * offset[c] for c in range(3)]
                sink_sum = [sink_sum[c] + force[c] for c in range(3)]
                total = [jnp.sum(force[c], axis=1, keepdims=True) for c in range(3)]
                source_sum.append(
                    jnp.where(
                        masks[0],
                        total[0],
                        jnp.where(masks[1], total[1], jnp.where(masks[2], total[2], 0.0)),
                    )
                )
            done.append((code >> 5 & 1, sink_block, k, sink_sum, source_sum))
        for g, sink_block, k, sink_sum, source_sum in done:
            for i, value in enumerate(source_sum):
                acc[g, pl.ds(8 * i, 8), :] -= value
            for c in range(3):
                row_force[sink_block, pl.ds(8 * c + k, 1), :] += jnp.sum(
                    sink_sum[c], axis=0, keepdims=True
                )

    fill(first_x, 0)
    fill(second_x, UNROLL)

    def turn(i, carry):
        first = i * (2 * UNROLL)
        use(first_x, first)
        fill(first_x, first + 2 * UNROLL)
        use(second_x, first + UNROLL)
        fill(second_x, first + 3 * UNROLL)
        return carry

    turns = every // (2 * UNROLL)
    lax.fori_loop(0, turns, turn, 0)
    done = turns * (2 * UNROLL)

    @pl.when(done < every)
    def _():
        use(first_x, done)

    @pl.when(done + UNROLL < every)
    def _():
        use(second_x, done + UNROLL)


def reduce_kernel(
    chips, group, row_force, acc, out,
    column_force, row_sum, row_in, column_in, swap_row,
    column_send, column_recv, row_send, row_recv, swap_send, swap_recv,
):
    sink, src, core, half, steps, rows = peers_of(chips, group)
    other = 1 - core
    across = lax.rem(sink + chips, 2 * chips)
    partner = (sink + 1 - 2 * core, src)
    column = [(moved(sink, chips, step), src) for step in steps]
    row = [
        (h, o, (across if h else sink, lax.rem(src + o, group)))
        for o in rows for h in (1, 0) if (h, o) != (0, 0)
    ]

    def turn_column():
        for g in range(chips // 8):
            turned = acc[g].T
            for h in range(4):
                column_force[g * 4 + h] = turned[32 * h : 32 * h + FORCES, :]

    greet([peer for h, o, peer in row] + column + [partner], turn_column)
    order = [(h, o) for h, o, peer in row] + [(0, 0)]
    blocks = [(lax.rem(half + h, 2) * group, lax.rem(src + o, group)) for h, o in order]
    swaps = [
        remote(
            row_force.at[other * 2 * group + line + at], swap_row.at[i],
            swap_send.at[i], swap_recv.at[i], partner,
        )
        for i, (line, at) in enumerate(blocks)
    ]
    sends = list(swaps)
    for copy in swaps:
        copy.start()
    for i, peer in enumerate(column):
        copy = remote(
            column_force.at[ringed(sink, chips, steps[i])], column_in.at[i],
            column_send.at[i], column_recv.at[i], peer,
        )
        copy.start()
        sends.append(copy)
    for i, (line, at) in enumerate(blocks):
        swaps[i].wait_recv()
        row_sum[i] = row_force[core * 2 * group + line + at] + swap_row[i]
        if i < len(row):
            copy = remote(row_sum.at[i], row_in.at[i], row_send.at[i], row_recv.at[i], row[i][2])
            copy.start()
            sends.append(copy)
    total = column_force[ringed(sink, chips, 0)] + row_sum[len(row)]
    for i in reversed(range(len(row))):
        remote(row_sum.at[0], row_in.at[i], row_send.at[i], row_recv.at[i], partner).wait_recv()
        total = total + row_in[i]
    for i in reversed(range(len(column))):
        remote(column_force.at[0], column_in.at[i], column_send.at[i], column_recv.at[i], partner).wait_recv()
        total = total + column_in[i]
    out[...] = total.reshape(3, LEAF_DEV, CELLS)
    for copy in sends:
        copy.wait_send()


def per_device(chips, group, leaf_pos, leaf_mass, pair_ids, pair_count):
    vmem = pl.BlockSpec(memory_space=pltpu.VMEM)
    smem = pl.BlockSpec(memory_space=pltpu.SMEM)
    hbm = pl.BlockSpec(memory_space=pltpu.HBM)
    dma = pltpu.SemaphoreType.DMA
    ring = chips // 2
    column, codes, rows, choose = pl.pallas_call(
        functools.partial(gather_kernel, chips, group),
        name="gather",
        out_shape=(
            jax.ShapeDtypeStruct((ring, 4, LEAF_DEV, CELLS), F32),
            jax.ShapeDtypeStruct((16, CELLS), jnp.int32),
            jax.ShapeDtypeStruct((4, group, 4, LEAF_DEV, CELLS), F32),
            jax.ShapeDtypeStruct((8, 96, 512), BF16),
        ),
        in_specs=[hbm] * 3 + [smem],
        out_specs=(vmem,) * 4,
        scratch_shapes=[
            pltpu.VMEM((4, 8, CELLS), jnp.int32),
            pltpu.VMEM((4, LEAF_DEV, CELLS), F32),
            pltpu.VMEM((1, 1, 2, PAIR_CAP), jnp.int32),
            dma((3,)),
            dma((ring - 1,)), dma((ring - 1,)),
            dma((2 * group - 1,)), dma((2 * group - 1,)),
            dma((2 * group - 1,)), dma((2 * group - 1,)),
            dma((4,)), dma((4,)),
        ],
        compiler_params=pltpu.CompilerParams(
            collective_id=0, has_side_effects=True, vmem_limit_bytes=16 << 20
        ),
    )(*(
        pltpu.with_memory_space_constraint(x, pltpu.HBM)
        for x in (jnp.transpose(leaf_pos, (1, 0, 2)), leaf_mass, pair_ids)
    ), pair_count)
    row_force, acc = pl.pallas_call(
        functools.partial(pair_kernel, group, ring),
        name="pairs",
        out_shape=(
            jax.ShapeDtypeStruct((4 * group, FORCES, CELLS), F32),
            jax.ShapeDtypeStruct((ring // 4, 128, CELLS), F32),
        ),
        in_specs=[smem, vmem, vmem, vmem],
        out_specs=(vmem, vmem),
        scratch_shapes=[
            pltpu.VMEM((ring, 128, 128), BF16),
            pltpu.VMEM((3, 4 * group, 3, LEAF_DEV, CELLS), F32),
            pltpu.VMEM((UNROLL, 128, 512), F32),
            pltpu.VMEM((UNROLL, 128, 512), F32),
        ],
        compiler_params=pltpu.CompilerParams(vmem_limit_bytes=40 << 20),
    )(codes, rows, column, choose)
    force = pl.pallas_call(
        functools.partial(reduce_kernel, chips, group),
        name="reduce",
        out_shape=jax.ShapeDtypeStruct((3, LEAF_DEV, CELLS), F32),
        in_specs=[vmem, vmem],
        out_specs=vmem,
        scratch_shapes=[
            pltpu.VMEM((ring, FORCES, CELLS), F32),
            pltpu.VMEM((2 * group, FORCES, CELLS), F32),
            pltpu.VMEM((2 * group - 1, FORCES, CELLS), F32),
            pltpu.VMEM((ring - 1, FORCES, CELLS), F32),
            pltpu.VMEM((2 * group, FORCES, CELLS), F32),
            dma((ring - 1,)), dma((ring - 1,)),
            dma((2 * group - 1,)), dma((2 * group - 1,)),
            dma((2 * group,)), dma((2 * group,)),
        ],
        compiler_params=pltpu.CompilerParams(
            collective_id=1, has_side_effects=True, vmem_limit_bytes=16 << 20
        ),
    )(row_force, acc)
    return jnp.transpose(force, (1, 0, 2))


def solution(mesh):
    return jax.shard_map(
        functools.partial(per_device, mesh.shape["sink"] // 2, mesh.shape["src"]),
        mesh=mesh,
        in_specs=(
            P(("sink", "src"), None, None),
            P(("sink", "src"), None),
            P("sink", "src", None, None),
            P("sink", "src"),
        ),
        out_specs=P(("sink", "src"), None, None),
        check_vma=False,
    )
```
